128 devices in a mesh: seq: 32 (over x, y, core), exp: 4 (over z).
Axes of the slice: x: 4, y: 4, z: 4, core: 2. Of those that a mesh axis runs over, the one named last changes fastest.
Arguments:
- query_states: bfloat16 [4096, 4096], P('seq', 'exp'), may hold values from -5 to 5
- key_states: bfloat16 [4096, 4096], P('seq', 'exp'), may hold values from -5 to 5
- value_states: bfloat16 [4096, 4096], P('seq', 'exp'), may hold values from -6 to 6
- selected: int32 [32, 3], replicated, may hold values from 0 to 30, as said below
- residual: bfloat16 [4096, 7168], P('seq', 'exp'), may hold values from -15 to 15
- out_weight: bfloat16 [32, 128, 7168], P('exp', 'seq'), may hold values from -0.25 to 0.25
- norm_gain: bfloat16 [7168], P('exp'), may hold values from 0.5 to 1.5
- w_gate: bfloat16 [128, 7168, 512], P(('seq', 'exp')), may hold values from -0.0625 to 0.0625
- w_up: bfloat16 [128, 7168, 512], P(('seq', 'exp')), may hold values from -0.0625 to 0.0625
- w_down: bfloat16 [128, 512, 7168], P(('seq', 'exp')), may hold values from -0.1875 to 0.1875
- routes: int32 [4096, 8], P('seq'), may hold values from 0 to 63, all different within a row; in each aligned block of 128 rows (0 to 127, 128 to 255, ...) at most 20 rows name the same one
- route_weights: bfloat16 [4096, 8], P('seq'), may hold values from 0.099609375 to 0.59765625
Outputs:
- layer_out: bfloat16 [4096, 7168], P('seq', 'exp')
The draws below stay inside these ranges and needn't reach their ends.
Inputs may be any that keep to these rules, and one draw needn't show every extreme that they name: `selected`: for a block b of at least 3, row b holds 3 different earlier blocks, among them b - 1; for b under 3, it holds every earlier block once and b itself in the remaining entries. `routes`: each row names 8 different experts; in each aligned block of 128 rows (the tokens of one index of seq) no expert is named by more than 20 rows.
All inputs are finite; a program needn't handle non-finite values.
Results may differ from the reference program's by a relative error of at most 0.02.
Values may be sent and summed in bfloat16 or wider, within the bound.
No kernel may reach another device: no remote copies, remote signals or barrier semaphores. Data moves between devices by JAX's collectives and lax.ppermute only.
A program may use at most 128 MiB of HBM per device.

```python
import math
import jax
import jax.numpy as jnp
import numpy as np
from jax import lax

D = 7168
HEADS = 32
HEAD_DIM = 128
FFN_HIDDEN = 1024
EXPERT_TOPK = 8
BLOCK_TOPK = 3
BLOCK = 128
CONTEXT = 4096
KV_BLOCK_COUNT = 32
EXPERTS = 64
CAP = 20
N_EXP = 4


def draw_query_states(key, part):
    key = jax.random.fold_in(key, 11)
    shape = (CONTEXT, HEADS * HEAD_DIM)
    values = jnp.clip(jax.random.normal(key, shape, jnp.float32), -5.0, 5.0)
    return values.astype(jnp.bfloat16)


def draw_key_states(key, part):
    key = jax.random.fold_in(key, 13)
    shape = (CONTEXT, HEADS * HEAD_DIM)
    values = jnp.clip(jax.random.normal(key, shape, jnp.float32), -5.0, 5.0)
    return values.astype(jnp.bfloat16)


def draw_residual(key, part):
    key = jax.random.fold_in(key, 31)
    columns = jnp.arange(D, dtype=jnp.float32)[None, :] / D
    column_scale = 0.5 * jnp.exp(columns * 1.0986123)
    row_scale = 10.0 ** jax.random.uniform(jax.random.fold_in(key, 1), (CONTEXT, 1), jnp.float32, -0.6, 0.4)
    base = jnp.clip(jax.random.normal(jax.random.fold_in(key, 3), (CONTEXT, D), jnp.float32), -4.0, 4.0)
    return (base * row_scale * column_scale).astype(jnp.bfloat16)


def draw_selected(key, part):
    key = jax.random.fold_in(key, 47)
    row_indices = jnp.arange(KV_BLOCK_COUNT, dtype=jnp.int32)[:, None]
    column_indices = jnp.arange(KV_BLOCK_COUNT, dtype=jnp.int32)[None, :]
    preference_boost = jax.random.randint(jax.random.fold_in(key, 1), (1, KV_BLOCK_COUNT), 0, 4)
    random_jitter = jax.random.randint(jax.random.fold_in(key, 2), (KV_BLOCK_COUNT, KV_BLOCK_COUNT), 0, 64)
    extra_boost = 48 * (preference_boost == 0).astype(jnp.int32) + 64 * (column_indices == 0).astype(jnp.int32) + 256 * (column_indices == row_indices - 1).astype(jnp.int32)
    block_score = (random_jitter + extra_boost) * KV_BLOCK_COUNT + column_indices
    block_score = jnp.where(column_indices < row_indices, block_score, -1 - column_indices)
    _, chosen = lax.top_k(block_score, BLOCK_TOPK)
    chosen = chosen.astype(jnp.int32)
    return jnp.where(chosen < row_indices, chosen, row_indices).astype(jnp.int32)


def levels(rng, extent, cuts, low, top_value):
    loudness, own = 1.0, jax.random.fold_in(rng, 6)
    for position, shards_of in cuts:
        draws = jnp.exp(jax.random.uniform(jax.random.fold_in(own, position), (shards_of,), jnp.float32, low / len(cuts), top_value / len(cuts)))
        loudness = loudness * jnp.repeat(draws, extent[position] // shards_of).reshape([-1 if axis == position else 1 for axis in range(len(extent))])
    return loudness


def shared_out(own_key, own, number, rows, count, top, limit, slope):
    sequence = jax.random.permutation(own_key, count)
    packed, usual = load_shares(count, rows * top, limit, slope, True), load_shares(count, rows * top, limit, slope, False)
    places = jnp.arange(count)

    def named(lengths, offset_by):
        used = int((lengths > 0).sum())
        fixed = max(1, used // 4)
        passed = fixed + (places - fixed + offset_by * (used - fixed)) % max(1, count - fixed)
        return jnp.zeros((count,), jnp.int32).at[sequence[jnp.where(places < fixed, places, passed)]].set(jnp.asarray(lengths, jnp.int32))

    lengths = jnp.where(number % 4 == 0, named(packed, number // 4), named(usual, number - number // 4 - 1))
    mixed = jax.random.permutation(jax.random.fold_in(own, 3), count)
    donor, sink = mixed[0:count // 2 * 2:2], mixed[1:count // 2 * 2:2]
    room = jnp.minimum(lengths[donor] - 1, limit - lengths[sink]) // 2
    room = jnp.where((donor == sequence[0]) | (sink == sequence[0]) | (lengths[sink] == 0), 0, jnp.maximum(room, 0))
    passed = jax.random.randint(jax.random.fold_in(own, 4), (count // 2,), 0, 1 << 20) % (room + 1)
    lengths = lengths.at[donor].add(-passed).at[sink].add(passed)
    labels = jnp.searchsorted(jnp.cumsum(lengths), jnp.arange(rows * top), side="right").astype(jnp.int32)
    listing = labels.reshape(top, rows).T
    listing = listing[jax.random.permutation(jax.random.fold_in(own, 1), rows)]
    offset_by = jax.random.randint(jax.random.fold_in(own, 2), (rows, 1), 0, top)
    return jnp.take_along_axis(listing, (jnp.arange(top)[None, :] + offset_by) % top, axis=1)


def load_shares(number_of, total, limit, slope, full):
    loads = [(1 << 20) // math.isqrt(rank ** slope) + 1 for rank in range(1, number_of + 1)]
    largest = limit if full else min(limit, max(-(-total // number_of), total * loads[0] // sum(loads)))
    least = 1 if total - largest >= number_of - 1 else 0
    counts, rest = [largest] + [least] * (number_of - 1), total - largest - least * (number_of - 1)
    while rest > 0:
        movable = [i for i in range(1, number_of) if counts[i] < largest] or [i for i in range(1, number_of) if counts[i] < limit]
        mass, left = sum([loads[i] for i in movable]), rest
        for i in movable:
            more = min(limit - counts[i], max(1, left * loads[i] // mass), rest)
            counts[i] = counts[i] + more
            rest = rest - more
    return np.array(counts)


def noise(rng, dims, width, bound, pieces=(), held_as=jnp.bfloat16):
    values = jax.random.normal(rng, dims, jnp.float32) * width
    if len(pieces) > 0:
        values = levels(rng, dims, pieces, -0.22, 0.18) * values
    return jnp.clip(values, min=-bound, max=bound).astype(held_as)


def setup_inputs(seed: int = 0) -> dict:
    key_of = jax.random.split(jax.random.key(seed), 13)
    query_states = draw_query_states(jax.random.fold_in(key_of[12], 71), 0)
    key_states = draw_key_states(jax.random.fold_in(key_of[12], 71), 0)
    value_states = noise(key_of[2], (CONTEXT, HEADS * HEAD_DIM), 1.0, 6.0, ((0, 32), (1, 4)))
    selected = draw_selected(jax.random.fold_in(key_of[12], 71), 0)
    residual = draw_residual(jax.random.fold_in(key_of[12], 71), 0)
    out_weight = noise(key_of[5], (HEADS, HEAD_DIM, D), (HEADS * HEAD_DIM // 8) ** -0.5, 0.25, ((0, 4), (1, 32)))
    norm_gain = jnp.clip(1.0 + 0.1 * jax.random.normal(key_of[6], (D,), jnp.float32), 0.5, 1.5).astype(jnp.bfloat16)
    w_gate = noise(key_of[7], (2 * EXPERTS, D, FFN_HIDDEN // 2), D ** -0.5, 0.0625, ((0, 128),))
    w_up = noise(key_of[8], (2 * EXPERTS, D, FFN_HIDDEN // 2), D ** -0.5, 0.0625, ((0, 128),))
    w_down = noise(key_of[9], (2 * EXPERTS, FFN_HIDDEN // 2, D), FFN_HIDDEN ** -0.5, 0.1875, ((0, 128),))
    routes_keys = jax.random.split(jax.random.fold_in(key_of[10], 1), CONTEXT // BLOCK)
    routes_turns = jax.random.permutation(jax.random.fold_in(key_of[10], 3), CONTEXT // BLOCK)
    routes = jax.vmap(lambda own, number: shared_out(jax.random.fold_in(key_of[10], 2), own, number, BLOCK, EXPERTS, EXPERT_TOPK, CAP, 2))(routes_keys, routes_turns).reshape((CONTEXT, EXPERT_TOPK))
    route_weights = jnp.clip(0.099609375 + 0.49804688 * jax.random.uniform(key_of[11], (CONTEXT, EXPERT_TOPK), jnp.float32) ** levels(key_of[11], (CONTEXT, EXPERT_TOPK), ((0, 32),), -0.2, 0.2), 0.099609375, 0.59765625).astype(jnp.bfloat16)
    return {"query_states": query_states, "key_states": key_states, "value_states": value_states, "selected": selected, "residual": residual, "out_weight": out_weight, "norm_gain": norm_gain, "w_gate": w_gate, "w_up": w_up, "w_down": w_down, "routes": routes, "route_weights": route_weights}


EPSILON = 1e-06
NEGATIVE = -1e+30

def attend_block(block_index, query_states, key_states, value_states, selected):
    feature_width = HEADS * HEAD_DIM
    first_row = block_index * BLOCK
    query_rows = lax.dynamic_slice_in_dim(query_states, first_row, BLOCK, 0).astype(jnp.float32).reshape(BLOCK, HEADS, HEAD_DIM)
    chosen = lax.dynamic_index_in_dim(selected, block_index, 0, keepdims=False)
    key_blocks = key_states.reshape(KV_BLOCK_COUNT, BLOCK, feature_width)
    value_blocks = value_states.reshape(KV_BLOCK_COUNT, BLOCK, feature_width)
    far_keys = jnp.take(key_blocks, chosen, axis=0).reshape(BLOCK_TOPK * BLOCK, feature_width)
    far_values = jnp.take(value_blocks, chosen, axis=0).reshape(BLOCK_TOPK * BLOCK, feature_width)
    own_keys = lax.dynamic_slice_in_dim(key_states, first_row, BLOCK, 0)
    own_values = lax.dynamic_slice_in_dim(value_states, first_row, BLOCK, 0)
    all_keys = jnp.concatenate([far_keys, own_keys], axis=0).astype(jnp.float32).reshape(-1, HEADS, HEAD_DIM)
    all_values = jnp.concatenate([far_values, own_values], axis=0).astype(jnp.float32).reshape(-1, HEADS, HEAD_DIM)
    scores = jnp.einsum('qhd,khd->hqk', query_rows, all_keys) * (1.0 / math.sqrt(HEAD_DIM))
    far_visible = jnp.repeat(chosen < block_index, BLOCK)
    positions = jnp.arange(BLOCK, dtype=jnp.int32)
    causal = positions[None, :] <= positions[:, None]
    visible = jnp.concatenate([jnp.broadcast_to(far_visible[None, :], (BLOCK, BLOCK_TOPK * BLOCK)), causal], axis=1)
    scores = jnp.where(visible[None], scores, NEGATIVE)
    row_peak = lax.optimization_barrier(jnp.max(scores, axis=2, keepdims=True))
    weights = jnp.exp(scores - row_peak)
    row_total = lax.optimization_barrier(jnp.sum(weights, axis=2, keepdims=True))
    soft_weights = (weights / row_total).astype(jnp.bfloat16)
    attended = jnp.einsum('hqk,khd->qhd', soft_weights.astype(jnp.float32), all_values)
    return attended.astype(jnp.bfloat16)

def reference(query_states, key_states, value_states, selected, residual, out_weight, norm_gain, w_gate, w_up, w_down, routes, route_weights):

    def one_block(block_index):
        return attend_block(block_index, query_states, key_states, value_states, selected)
    attention = lax.map(one_block, jnp.arange(KV_BLOCK_COUNT, dtype=jnp.int32)).reshape(CONTEXT, HEADS * HEAD_DIM)
    heads_here = HEADS // N_EXP
    span = heads_here * HEAD_DIM
    stream = residual.astype(jnp.float32)
    for group in range(N_EXP):
        head_cols = attention[:, group * span:(group + 1) * span]
        weight = out_weight[group * heads_here:(group + 1) * heads_here].reshape(span, D)
        group_term = jnp.dot(head_cols, weight, preferred_element_type=jnp.float32).astype(jnp.bfloat16)
        group_term = lax.optimization_barrier(group_term)
        stream = stream + group_term.astype(jnp.float32)
    hidden = stream.astype(jnp.bfloat16)
    hidden_wide = hidden.astype(jnp.float32)
    rms_scale = lax.rsqrt(lax.optimization_barrier(jnp.mean(hidden_wide * hidden_wide, axis=1, keepdims=True)) + EPSILON)
    normed = (hidden_wide * rms_scale * norm_gain.astype(jnp.float32)[None, :]).astype(jnp.bfloat16)
    per_expert = KV_BLOCK_COUNT * CAP
    flat_routes = routes.reshape(KV_BLOCK_COUNT, BLOCK * EXPERT_TOPK)
    expert_hits = (flat_routes[:, :, None] == jnp.arange(EXPERTS, dtype=jnp.int32)[None, None, :]).astype(jnp.int32)
    slot_rank = lax.optimization_barrier(jnp.sum((jnp.cumsum(expert_hits, axis=1) - expert_hits) * expert_hits, axis=2))
    slot_index = (flat_routes * per_expert + jnp.arange(KV_BLOCK_COUNT, dtype=jnp.int32)[:, None] * CAP + slot_rank).reshape(-1)
    token_of = (jnp.arange(CONTEXT * EXPERT_TOPK, dtype=jnp.int32) // EXPERT_TOPK).astype(jnp.int32)
    token_table = jnp.full((EXPERTS * per_expert,), -1, jnp.int32).at[slot_index].set(token_of)
    weight_table = jnp.zeros((EXPERTS * per_expert,), jnp.bfloat16).at[slot_index].set(route_weights.reshape(-1))

    def one_expert(running, expert):
        tokens_in = lax.dynamic_slice_in_dim(token_table, expert * per_expert, per_expert)
        factors = lax.dynamic_slice_in_dim(weight_table, expert * per_expert, per_expert).astype(jnp.float32)
        occupied = tokens_in >= 0
        safe_index = jnp.maximum(tokens_in, 0)
        expert_rows = jnp.where(occupied[:, None], jnp.take(normed, safe_index, axis=0), jnp.zeros((), normed.dtype))
        pair_sum = jnp.zeros((per_expert, D), jnp.float32)
        for half_index in range(2):
            weight_row = expert * 2 + half_index
            gate_matrix = lax.dynamic_index_in_dim(w_gate, weight_row, 0, keepdims=False)
            up_matrix = lax.dynamic_index_in_dim(w_up, weight_row, 0, keepdims=False)
            down_matrix = lax.dynamic_index_in_dim(w_down, weight_row, 0, keepdims=False)
            gate_values = jnp.dot(expert_rows, gate_matrix, preferred_element_type=jnp.float32)
            up_values = jnp.dot(expert_rows, up_matrix, preferred_element_type=jnp.float32)
            active = (jax.nn.silu(gate_values) * up_values).astype(jnp.bfloat16)
            half_out = jnp.dot(active, down_matrix, preferred_element_type=jnp.float32).astype(jnp.bfloat16)
            half_out = lax.optimization_barrier(half_out)
            pair_sum = pair_sum + half_out.astype(jnp.float32)
        pair_out = lax.optimization_barrier(pair_sum.astype(jnp.bfloat16))
        running = running.at[safe_index].add(factors[:, None] * pair_out.astype(jnp.float32))
        return (running, None)
    expert_term, _ = lax.scan(one_expert, jnp.zeros((CONTEXT, D), jnp.float32), jnp.arange(EXPERTS, dtype=jnp.int32))
    return (hidden_wide + expert_term).astype(jnp.bfloat16)
```

```python
import math

import jax
import jax.numpy as jnp
from jax import lax
from jax.sharding import PartitionSpec as P

EPSILON = 1e-06
NEGATIVE = -1e30
CAP = 20
DIRECT = 4
CHUNK = (CAP - DIRECT) // 2
BF16 = jnp.bfloat16
F32 = jnp.float32


def dot(a, b):
    return jnp.dot(a, b, preferred_element_type=F32)


def dot_rows(a, b):
    return lax.dot_general(a, b, (((0,), (0,)), ((), ())), preferred_element_type=F32)


def half_swap(block):
    return lax.ppermute(block, "exp", [(i, i ^ 1) for i in range(4)])


def group_swap(block):
    return lax.ppermute(block, "exp", [(i, 3 - i) for i in range(4)])


def spread(block):
    return lax.all_to_all(block, "seq", split_axis=0, concat_axis=0, tiled=True)


def fetch_blocks(key_states, value_states, selected):
    count = lax.axis_size("seq")
    rows, width = key_states.shape
    piece = rows // count
    stacked = jnp.stack([key_states, value_states])
    previous = lax.ppermute(stacked, "seq", [(i, i + 1) for i in range(count - 1)])
    pieces = lax.all_to_all(
        stacked.reshape(2, count, piece, width), "seq", split_axis=1, concat_axis=1, tiled=True
    )
    before = jnp.arange(count, dtype=jnp.int32)[:, None] - 1
    place = jnp.argmax(selected == before, axis=1)
    first = jnp.where(place == 0, selected[:, 1], selected[:, 0])
    second = jnp.where(place == 2, selected[:, 1], selected[:, 2])
    others = jnp.stack([first, second])
    wanted = jnp.take(pieces, others, axis=1)
    fetched = lax.all_to_all(wanted, "seq", split_axis=2, concat_axis=2, tiled=True)
    return fetched.reshape(2, 2 * rows, width), previous, others


def attend(query_states, key_states, value_states, selected, heads):
    position = lax.axis_index("seq")
    rows, width = query_states.shape
    head_dim = width // heads
    fetched, previous, others = fetch_blocks(key_states, value_states, selected)
    keys = jnp.concatenate([fetched[0], previous[0], key_states], axis=0)
    values = jnp.concatenate([fetched[1], previous[1], value_states], axis=0)
    keys = keys.reshape(-1, heads, head_dim)
    values = values.reshape(-1, heads, head_dim)
    queries = query_states.reshape(rows, heads, head_dim)
    scores = jnp.einsum("qhd,khd->hqk", queries, keys, preferred_element_type=F32) * (
        1.0 / math.sqrt(head_dim)
    )
    mine = lax.dynamic_slice_in_dim(others, position, 1, 1)[:, 0]
    far = jnp.concatenate([mine < position, (position > 0)[None]])
    far = jnp.repeat(far, rows)
    places = jnp.arange(rows, dtype=jnp.int32)
    causal = places[None, :] <= places[:, None]
    visible = jnp.concatenate(
        [jnp.broadcast_to(far[None, :], (rows, far.shape[0])), causal], axis=1
    )
    scores = jnp.where(visible[None], scores, NEGATIVE)
    peak = jnp.max(scores, axis=2, keepdims=True)
    weights = jnp.exp(scores - peak)
    total = jnp.sum(weights, axis=2, keepdims=True)
    soft_weights = (weights / total).astype(BF16)
    attended = jnp.einsum("hqk,khd->qhd", soft_weights, values, preferred_element_type=F32)
    return attended.astype(BF16).reshape(rows, width)


def regroup(attended, heads, pieces):
    width = attended.shape[1]
    head_dim = width // heads
    piece = head_dim // pieces
    old = jnp.arange(width, dtype=jnp.int32)
    new_of_old = (old % head_dim) // piece * (heads * piece) + old // head_dim * piece + old % piece
    move = (new_of_old[:, None] == jnp.arange(width, dtype=jnp.int32)[None, :]).astype(BF16)
    return dot(attended, move).astype(BF16)


def sum_slices(projected, width):
    exp = lax.axis_index("exp")
    total = None
    for shift in (2, 1, 3, 0):
        target = (exp + shift) % 4
        block = lax.dynamic_slice_in_dim(projected, target * width, width, 1)
        if shift:
            block = lax.ppermute(block, "exp", [(i, (i + shift) % 4) for i in range(4)])
        block = block.astype(F32)
        total = block if total is None else total + block
    return total


def per_device(
    query_states,
    key_states,
    value_states,
    selected,
    residual,
    out_weight,
    norm_gain,
    w_gate,
    w_up,
    w_down,
    routes,
    route_weights,
):
    count = lax.axis_size("seq")
    exp = lax.axis_index("exp")
    rows, width = residual.shape
    heads = out_weight.shape[0]
    model_width = 4 * width
    group = exp // 2
    side = (exp >= 2).astype(jnp.int32)
    half = jnp.where(jnp.logical_or(exp == 0, exp == 3), 0, 1)
    other = 1 - half

    def halves(block, which, axis):
        low = lax.dynamic_slice_in_dim(block, which * width, width, axis)
        high = lax.dynamic_slice_in_dim(block, (3 - which) * width, width, axis)
        return jnp.concatenate([low, high], axis=axis)

    down_mine = halves(w_down[0], half, 1)
    down_theirs = half_swap(halves(w_down[0], other, 1))
    full_out = lax.all_gather(out_weight.reshape(-1, model_width), "seq", axis=0, tiled=True)
    gate_up_mine = jnp.concatenate([halves(w_gate[0], half, 0), halves(w_up[0], half, 0)], axis=1)
    gate_up_theirs = jnp.concatenate(
        [halves(w_gate[0], other, 0), halves(w_up[0], other, 0)], axis=1
    )
    gain_theirs = group_swap(norm_gain)

    experts = 2 * jnp.arange(count, dtype=jnp.int32) + group
    named = routes.T[:, None, :] == experts[None, :, None]
    hits = jnp.any(named, axis=0)
    token_weight = jnp.sum(jnp.where(named, route_weights.T[:, None, :].astype(F32), 0.0), axis=0)
    steps = jnp.arange(rows, dtype=jnp.int32)
    earlier = (steps[:, None] < steps[None, :]).astype(BF16)
    rank = jnp.where(hits, dot(hits.astype(BF16), earlier).astype(jnp.int32), -1)

    def slots(first, number):
        ids = first + jnp.arange(number, dtype=jnp.int32)
        return rank[:, None, :] == ids[None, :, None]

    def picker(mask):
        return mask.astype(BF16).reshape(-1, mask.shape[-1])

    def weigher(mask):
        return jnp.where(mask, token_weight[:, None, :], 0.0).astype(BF16).reshape(-1, rows)

    masks = [slots(0, CHUNK), slots(CHUNK, CHUNK)]
    last = slots(CAP - DIRECT, DIRECT)
    empty = jnp.zeros_like(last)
    last_low = jnp.concatenate([last, empty], axis=1)
    last_high = jnp.concatenate([empty, last], axis=1)

    attended = attend(query_states, key_states, value_states, selected, heads)
    attended = regroup(attended, heads, count)
    projected = dot(attended, full_out).astype(BF16)
    hidden = (sum_slices(projected, width) + residual.astype(F32)).astype(BF16)
    wide = hidden.astype(F32)
    hidden_theirs = group_swap(hidden)
    squares = lax.psum(jnp.sum(wide * wide, axis=1), "exp")
    scale = lax.rsqrt(squares / model_width + EPSILON)[:, None]
    normed_mine = (wide * scale * norm_gain.astype(F32)[None, :]).astype(BF16)
    normed_theirs = (
        hidden_theirs.astype(F32) * scale * gain_theirs.astype(F32)[None, :]
    ).astype(BF16)
    lower = side == 0
    normed = jnp.concatenate(
        [jnp.where(lower, normed_mine, normed_theirs), jnp.where(lower, normed_theirs, normed_mine)],
        axis=1,
    )
    normed_other = half_swap(normed)

    received = [spread(dot(picker(mask), normed).astype(BF16)) for mask in masks]
    both = jnp.concatenate([normed, normed_other], axis=0)
    pick_last = jnp.concatenate([picker(last_low), picker(last_high)], axis=1)
    received_last = spread(dot(pick_last, both).astype(BF16))

    compact = jnp.arange(count * DIRECT, dtype=jnp.int32)
    low_row = compact // DIRECT * 2 * DIRECT + compact % DIRECT
    packed = jnp.arange(2 * count * DIRECT, dtype=jnp.int32)
    take_low = (low_row[:, None] == packed[None, :]).astype(BF16)
    take_high = (low_row[:, None] + DIRECT == packed[None, :]).astype(BF16)

    def hidden_units(mine, theirs):
        values = dot(mine, gate_up_mine) + dot(theirs, gate_up_theirs)
        units = values.shape[1] // 2
        gate, up = values[:, :units], values[:, units:]
        return (jax.nn.silu(gate) * up).astype(BF16)

    def expert_out(act):
        return (dot(act, down_mine) + dot(half_swap(act), down_theirs)).astype(BF16)

    outs = [spread(expert_out(hidden_units(block, half_swap(block)))) for block in received]
    last_out = expert_out(
        hidden_units(
            dot(take_low, received_last).astype(BF16), dot(take_high, received_last).astype(BF16)
        )
    )
    last_out = spread(
        (dot_rows(take_low, last_out[:, :width]) + dot_rows(take_high, last_out[:, width:])).astype(
            BF16
        )
    )

    combined = sum(dot_rows(weigher(mask), block) for mask, block in zip(masks, outs))
    combined_last = jnp.concatenate(
        [dot_rows(weigher(last_low), last_out), dot_rows(weigher(last_high), last_out)], axis=1
    )
    combined = combined + combined_last
    keep = lax.dynamic_slice_in_dim(combined, side * width, width, 1)
    give = lax.dynamic_slice_in_dim(combined, (1 - side) * width, width, 1).astype(BF16)
    return (wide + (keep + group_swap(give).astype(F32))).astype(BF16)


def solution(mesh):
    return jax.shard_map(
        per_device,
        mesh=mesh,
        in_specs=(
            P("seq", "exp"),
            P("seq", "exp"),
            P("seq", "exp"),
            P(),
            P("seq", "exp"),
            P("exp", "seq", None),
            P("exp"),
            P(("seq", "exp"), None, None),
            P(("seq", "exp"), None, None),
            P(("seq", "exp"), None, None),
            P("seq", None),
            P("seq", None),
        ),
        out_specs=P("seq", "exp"),
        check_vma=False,
    )
```

```python
import math

import jax
import jax.numpy as jnp
from jax import lax
from jax.sharding import PartitionSpec as P

EPSILON = 1e-06
NEGATIVE = -1e30
CAP = 20
DIRECT = 4
CHUNK = (CAP - DIRECT) // 2
BF16 = jnp.bfloat16
F32 = jnp.float32


def dot(a, b):
    return jnp.dot(a, b, preferred_element_type=F32)


def dot_rows(a, b):
    return lax.dot_general(a, b, (((0,), (0,)), ((), ())), preferred_element_type=F32)


def half_swap(block):
    return lax.ppermute(block, "exp", [(i, i ^ 1) for i in range(4)])


def group_swap(block):
    return lax.ppermute(block, "exp", [(i, 3 - i) for i in range(4)])


def spread(block):
    return lax.all_to_all(block, "seq", split_axis=0, concat_axis=0, tiled=True)


def fetch_blocks(key_states, value_states, selected):
    count = lax.axis_size("seq")
    rows, width = key_states.shape
    piece = 2 * rows // count
    stacked = jnp.concatenate([key_states, value_states], axis=0)
    pieces = spread(stacked).reshape(count, piece, width)
    previous = lax.ppermute(stacked, "seq", [(i, i + 1) for i in range(count - 1)])
    before = jnp.arange(count, dtype=jnp.int32)[:, None] - 1
    place = jnp.argmax(selected == before, axis=1)
    first = jnp.where(place == 0, selected[:, 1], selected[:, 0])
    second = jnp.where(place == 2, selected[:, 1], selected[:, 2])
    others = jnp.stack([first, second], axis=1)
    wanted = jnp.take(pieces, others.reshape(-1), axis=0).reshape(-1, width)
    fetched = spread(wanted)
    return fetched, previous, others


def attend(query_states, key_states, value_states, selected, heads):
    position = lax.axis_index("seq")
    rows, width = query_states.shape
    head_dim = width // heads
    fetched, previous, others = fetch_blocks(key_states, value_states, selected)
    keys = jnp.concatenate([fetched[: 2 * rows], previous[:rows], key_states], axis=0)
    values = jnp.concatenate([fetched[2 * rows :], previous[rows:], value_states], axis=0)
    keys = keys.reshape(-1, heads, head_dim)
    values = values.reshape(-1, heads, head_dim)
    queries = query_states.reshape(rows, heads, head_dim)
    scores = jnp.einsum("qhd,khd->hqk", queries, keys, preferred_element_type=F32) * (
        1.0 / math.sqrt(head_dim)
    )
    mine = lax.dynamic_slice_in_dim(others, position, 1, 0)[0] < position
    turn = jnp.arange(2 * rows, dtype=jnp.int32) // (2 * rows // lax.axis_size("seq")) % 2
    far = jnp.where(turn == 0, mine[0], mine[1])
    far = jnp.concatenate([far, jnp.broadcast_to(position > 0, (rows,))])
    places = jnp.arange(rows, dtype=jnp.int32)
    causal = places[None, :] <= places[:, None]
    visible = jnp.concatenate(
        [jnp.broadcast_to(far[None, :], (rows, far.shape[0])), causal], axis=1
    )
    scores = jnp.where(visible[None], scores, NEGATIVE)
    peak = jnp.max(scores, axis=2, keepdims=True)
    weights = jnp.exp(scores - peak)
    total = jnp.sum(weights, axis=2, keepdims=True)
    soft_weights = (weights / total).astype(BF16)
    attended = jnp.einsum("hqk,khd->qhd", soft_weights, values, preferred_element_type=F32)
    return attended.astype(BF16).reshape(rows, width)


def regroup(attended, heads, pieces):
    width = attended.shape[1]
    head_dim = width // heads
    piece = head_dim // pieces
    old = jnp.arange(width, dtype=jnp.int32)
    new_of_old = (old % head_dim) // piece * (heads * piece) + old // head_dim * piece + old % piece
    move = (new_of_old[:, None] == jnp.arange(width, dtype=jnp.int32)[None, :]).astype(BF16)
    return dot(attended, move).astype(BF16)


def project_sum(attended, full_out, width):
    exp = lax.axis_index("exp")
    total = None
    for shift in (2, 1, 3, 0):
        target = (exp + shift) % 4
        columns = lax.dynamic_slice_in_dim(full_out, target * width, width, 1)
        block = dot(attended, columns).astype(BF16)
        if shift:
            block = lax.ppermute(block, "exp", [(i, (i + shift) % 4) for i in range(4)])
        block = block.astype(F32)
        total = block if total is None else total + block
    return total


def per_device(
    query_states,
    key_states,
    value_states,
    selected,
    residual,
    out_weight,
    norm_gain,
    w_gate,
    w_up,
    w_down,
    routes,
    route_weights,
):
    count = lax.axis_size("seq")
    exp = lax.axis_index("exp")
    rows, width = residual.shape
    heads = out_weight.shape[0]
    model_width = 4 * width
    group = exp // 2
    side = (exp >= 2).astype(jnp.int32)
    half = jnp.where(jnp.logical_or(exp == 0, exp == 3), 0, 1)
    other = 1 - half

    def ordered(mine, theirs):
        lower = side == 0
        return jnp.concatenate(
            [jnp.where(lower, mine, theirs), jnp.where(lower, theirs, mine)], axis=1
        )

    def halves(block, which, axis):
        low = lax.dynamic_slice_in_dim(block, which * width, width, axis)
        high = lax.dynamic_slice_in_dim(block, (3 - which) * width, width, axis)
        return jnp.concatenate([low, high], axis=axis)

    down_mine = halves(w_down[0], half, 1)
    down_theirs = half_swap(halves(w_down[0], other, 1))
    full_out = lax.all_gather(out_weight.reshape(-1, model_width), "seq", axis=0, tiled=True)
    gain = norm_gain[None, :]
    gain_mine = ordered(gain, group_swap(gain))
    gain_theirs = half_swap(gain_mine)

    experts = 2 * jnp.arange(count, dtype=jnp.int32) + group
    named = routes.T[:, None, :] == experts[None, :, None]
    hits = jnp.any(named, axis=0)
    token_weight = jnp.sum(jnp.where(named, route_weights.T[:, None, :].astype(F32), 0.0), axis=0)
    steps = jnp.arange(rows, dtype=jnp.int32)
    earlier = (steps[:, None] < steps[None, :]).astype(BF16)
    rank = jnp.where(hits, dot(hits.astype(BF16), earlier).astype(jnp.int32), -1)

    def slots(first, number):
        ids = first + jnp.arange(number, dtype=jnp.int32)
        return rank[:, None, :] == ids[None, :, None]

    def picker(mask):
        return mask.astype(BF16).reshape(-1, mask.shape[-1])

    def weigher(mask):
        return jnp.where(mask, token_weight[:, None, :], 0.0).astype(BF16).reshape(-1, rows)

    masks = [slots(0, CHUNK), slots(CHUNK, CHUNK)]
    last = slots(CAP - DIRECT, DIRECT)
    empty = jnp.zeros_like(last)
    last_low = jnp.concatenate([last, empty], axis=1)
    last_high = jnp.concatenate([empty, last], axis=1)

    attended = attend(query_states, key_states, value_states, selected, heads)
    attended = regroup(attended, heads, count)
    hidden = (project_sum(attended, full_out, width) + residual.astype(F32)).astype(BF16)
    wide = hidden.astype(F32)
    gained = (wide * gain.astype(F32)).astype(BF16)
    gained, down_theirs = lax.optimization_barrier((gained, down_theirs))
    gained = ordered(gained, group_swap(gained))
    gained_other = half_swap(gained)

    received = []
    for mask in masks:
        rows_out = dot(picker(mask), gained).astype(BF16)
        if received:
            rows_out, received[-1] = lax.optimization_barrier((rows_out, received[-1]))
        received.append(spread(rows_out))
    both = jnp.concatenate([gained, gained_other], axis=0)
    pick_last = jnp.concatenate([picker(last_low), picker(last_high)], axis=1)
    rows_out = dot(pick_last, both).astype(BF16)
    rows_out, received[-1] = lax.optimization_barrier((rows_out, received[-1]))
    received_last = spread(rows_out)

    compact = jnp.arange(count * DIRECT, dtype=jnp.int32)
    low_row = compact // DIRECT * 2 * DIRECT + compact % DIRECT
    packed = jnp.arange(2 * count * DIRECT, dtype=jnp.int32)
    take_low = (low_row[:, None] == packed[None, :]).astype(BF16)
    take_high = (low_row[:, None] + DIRECT == packed[None, :]).astype(BF16)

    def part(block, which, gain_half):
        values = []
        for weight in (w_gate[0], w_up[0]):
            low = lax.dynamic_slice_in_dim(weight, which * width, width, 0)
            high = lax.dynamic_slice_in_dim(weight, (3 - which) * width, width, 0)
            values.append(dot(block[:, :width], low) + dot(block[:, width:], high))
        plain = block.astype(F32) / gain_half.astype(F32)
        return values + [jnp.sum(plain * plain, axis=1, keepdims=True)]

    def hidden_units(mine, theirs):
        parts = zip(part(mine, half, gain_mine), part(theirs, other, gain_theirs))
        gate, up, squares = (a + b for a, b in parts)
        scale = lax.rsqrt(squares / model_width + EPSILON)
        return (jax.nn.silu(gate * scale) * (up * scale)).astype(BF16)

    def expert_out(act):
        return (dot(act, down_mine) + dot(half_swap(act), down_theirs)).astype(BF16)

    swapped = [half_swap(block) for block in received]
    first_out = expert_out(hidden_units(received[0], swapped[0]))
    first_out, received_last = lax.optimization_barrier((first_out, received_last))
    first_out = spread(first_out)
    last_out = expert_out(
        hidden_units(
            dot(take_low, received_last).astype(BF16), dot(take_high, received_last).astype(BF16)
        )
    )
    last_out = (
        dot_rows(take_low, last_out[:, :width]) + dot_rows(take_high, last_out[:, width:])
    ).astype(BF16)
    last_out, first_out, swapped[1] = lax.optimization_barrier((last_out, first_out, swapped[1]))
    last_out = spread(last_out)
    second_out = expert_out(hidden_units(received[1], swapped[1]))
    second_out, last_out = lax.optimization_barrier((second_out, last_out))
    outs = [first_out, spread(second_out)]

    combined = sum(dot_rows(weigher(mask), block) for mask, block in zip(masks, outs))
    combined_last = jnp.concatenate(
        [dot_rows(weigher(last_low), last_out), dot_rows(weigher(last_high), last_out)], axis=1
    )
    combined = combined + combined_last
    keep = lax.dynamic_slice_in_dim(combined, side * width, width, 1)
    give = lax.dynamic_slice_in_dim(combined, (1 - side) * width, width, 1).astype(BF16)
    return (wide + (keep + group_swap(give).astype(F32))).astype(BF16)


def solution(mesh):
    return jax.shard_map(
        per_device,
        mesh=mesh,
        in_specs=(
            P("seq", "exp"),
            P("seq", "exp"),
            P("seq", "exp"),
            P(),
            P("seq", "exp"),
            P("exp", "seq", None),
            P("exp"),
            P(("seq", "exp"), None, None),
            P(("seq", "exp"), None, None),
            P(("seq", "exp"), None, None),
            P("seq", None),
            P("seq", None),
        ),
        out_specs=P("seq", "exp"),
        check_vma=False,
    )
```

```python
import math

import jax
import jax.numpy as jnp
from jax import lax
from jax.experimental import pallas as pl
from jax.experimental.pallas import tpu as pltpu
from jax.sharding import PartitionSpec as P

EPSILON = 1e-06
NEGATIVE = -1e30
CAP = 20
DIRECT = 12
SWAPPED = CAP - DIRECT
STEP = 1792
OUT_STEP = 896
MIB = 2**20
BF16 = jnp.bfloat16
F32 = jnp.float32


def dot(a, b):
    return jnp.dot(a, b, preferred_element_type=F32)


def dot_rows(a, b):
    return lax.dot_general(a, b, (((0,), (0,)), ((), ())), preferred_element_type=F32)


def half_swap(block):
    return lax.ppermute(block, "exp", [(i, i ^ 1) for i in range(4)])


def group_swap(block):
    return lax.ppermute(block, "exp", [(i, 3 - i) for i in range(4)])


def spread(block):
    return lax.all_to_all(block, "seq", split_axis=0, concat_axis=0, tiled=True)


def fetch_blocks(key_states, value_states, selected):
    count = lax.axis_size("seq")
    rows, width = key_states.shape
    piece = 2 * rows // count
    stacked = jnp.concatenate([key_states, value_states], axis=0)
    pieces = spread(stacked).reshape(count, piece, width)
    previous = lax.ppermute(stacked, "seq", [(i, i + 1) for i in range(count - 1)])
    before = jnp.arange(count, dtype=jnp.int32)[:, None] - 1
    place = jnp.argmax(selected == before, axis=1)
    first = jnp.where(place == 0, selected[:, 1], selected[:, 0])
    second = jnp.where(place == 2, selected[:, 1], selected[:, 2])
    others = jnp.stack([first, second], axis=1)
    wanted = jnp.take(pieces, others.reshape(-1), axis=0).reshape(-1, width)
    fetched = spread(wanted)
    return fetched, previous, others


def attend(query_states, key_states, value_states, selected, heads):
    position = lax.axis_index("seq")
    rows, width = query_states.shape
    head_dim = width // heads
    fetched, previous, others = fetch_blocks(key_states, value_states, selected)
    keys = jnp.concatenate([fetched[: 2 * rows], previous[:rows], key_states], axis=0)
    values = jnp.concatenate([fetched[2 * rows :], previous[rows:], value_states], axis=0)
    keys = keys.reshape(-1, heads, head_dim)
    values = values.reshape(-1, heads, head_dim)
    queries = query_states.reshape(rows, heads, head_dim)
    scores = jnp.einsum("qhd,khd->hqk", queries, keys, preferred_element_type=F32) * (
        1.0 / math.sqrt(head_dim)
    )
    mine = lax.dynamic_slice_in_dim(others, position, 1, 0)[0] < position
    turn = jnp.arange(2 * rows, dtype=jnp.int32) // (2 * rows // lax.axis_size("seq")) % 2
    far = jnp.where(turn == 0, mine[0], mine[1])
    far = jnp.concatenate([far, jnp.broadcast_to(position > 0, (rows,))])
    places = jnp.arange(rows, dtype=jnp.int32)
    causal = places[None, :] <= places[:, None]
    visible = jnp.concatenate(
        [jnp.broadcast_to(far[None, :], (rows, far.shape[0])), causal], axis=1
    )
    scores = jnp.where(visible[None], scores, NEGATIVE)
    peak = jnp.max(scores, axis=2, keepdims=True)
    weights = jnp.exp(scores - peak)
    total = jnp.sum(weights, axis=2, keepdims=True)
    soft_weights = (weights / total).astype(BF16)
    attended = jnp.einsum("hqk,khd->qhd", soft_weights, values, preferred_element_type=F32)
    return attended.astype(BF16).reshape(rows, width)


def regroup(attended, heads, pieces):
    width = attended.shape[1]
    head_dim = width // heads
    piece = head_dim // pieces
    old = jnp.arange(width, dtype=jnp.int32)
    new_of_old = (old % head_dim) // piece * (heads * piece) + old // head_dim * piece + old % piece
    move = (new_of_old[:, None] == jnp.arange(width, dtype=jnp.int32)[None, :]).astype(BF16)
    return dot(attended, move).astype(BF16)


def project_sum(attended, full_out, order, theirs_order, width):
    def product(index):
        columns = lax.dynamic_slice_in_dim(full_out, index * width, width, 1)
        return dot(attended, columns).astype(BF16)

    given = [half_swap(product(theirs_order[n])) for n in range(2)]
    kept = [product(order[n]) for n in range(2)]
    pairs = [(a.astype(F32) + b.astype(F32)).astype(BF16) for a, b in zip(kept, given)]
    return jnp.concatenate(
        [pair.astype(F32) + group_swap(pair).astype(F32) for pair in pairs], axis=1
    )


def lane_sums(block):
    total = block[:, :128]
    for low in range(128, block.shape[1], 128):
        total = total + block[:, low : low + 128]
    return total


def gated(gate, up):
    return (gate / (1.0 + jnp.exp(-gate)) * up).astype(BF16)


def call(kernel, vmem, order, steps, in_specs, out_specs, out_shape, scratch, *args):
    return pl.pallas_call(
        kernel,
        grid_spec=pltpu.PrefetchScalarGridSpec(
            num_scalar_prefetch=1,
            grid=(steps,),
            in_specs=in_specs,
            out_specs=out_specs,
            scratch_shapes=scratch,
        ),
        out_shape=out_shape,
        compiler_params=pltpu.CompilerParams(
            dimension_semantics=("arbitrary",), vmem_limit_bytes=vmem * MIB
        ),
        cost_estimate=pl.CostEstimate(flops=1000, bytes_accessed=1000, transcendentals=0),
    )(order, *args)


def whole(shape):
    return pl.BlockSpec(shape, lambda k, order: (0,) * len(shape))


def weight_rows(per_slice, units):
    return pl.BlockSpec(
        (1, STEP, units), lambda k, order: (0, order[k // per_slice] * per_slice + k % per_slice, 0)
    )


def half_units(block, gain_half, order, w_gate, w_up, before=None):
    rows, width = block.shape
    units = w_gate.shape[2]
    steps = width // STEP

    def kernel(order_ref, x_ref, gain_ref, wg_ref, wu_ref, *refs):
        k = pl.program_id(0)
        if before is None:
            gate_ref, up_ref, square_ref = refs
        else:
            gate_in, up_in, square_in, act_ref, gate_ref, up_ref, square_ref = refs

        @pl.when(k == 0)
        def _():
            for ref, start in zip(
                (gate_ref, up_ref, square_ref), (None,) * 3 if before is None else refs[:3]
            ):
                ref[...] = jnp.zeros_like(ref) if start is None else start[...]

        x = x_ref[...]
        gate_ref[...] += dot(x, wg_ref[0])
        up_ref[...] += dot(x, wu_ref[0])
        plain = x.astype(F32) * (1.0 / gain_ref[...].astype(F32))
        square_ref[...] += lane_sums(plain * plain)
        if before is not None:

            @pl.when(k == steps - 1)
            def _():
                total = jnp.sum(square_ref[...], axis=1, keepdims=True)
                scale = lax.rsqrt(total / (2 * width) + EPSILON)
                act_ref[...] = gated(gate_ref[...] * scale, up_ref[...] * scale)

    per_slice = steps // 2
    in_specs = [
        pl.BlockSpec((rows, STEP), lambda k, order: (0, k)),
        pl.BlockSpec((1, STEP), lambda k, order: (0, k)),
        weight_rows(per_slice, units),
        weight_rows(per_slice, units),
    ]
    sums = [(rows, units), (rows, units), (rows, 128)]
    args = [block, gain_half, w_gate, w_up]
    if before is None:
        return call(
            kernel,
            20,
            order,
            steps,
            in_specs,
            [whole(shape) for shape in sums],
            [jax.ShapeDtypeStruct(shape, F32) for shape in sums],
            [],
            *args,
        )
    return call(
        kernel,
        20,
        order,
        steps,
        in_specs + [whole(shape) for shape in sums],
        whole((rows, units)),
        jax.ShapeDtypeStruct((rows, units), BF16),
        [pltpu.VMEM(shape, F32) for shape in sums],
        *args,
        *before,
    )


def spreader(slots, groups, high):
    row = jnp.arange(groups * slots, dtype=jnp.int32)
    place = row // slots * 2 * slots + row % slots + (slots if high else 0)
    return (place[:, None] == jnp.arange(groups * 2 * slots, dtype=jnp.int32)[None, :]).astype(BF16)


def packed_units(block, slots, groups, order, w_gate, w_up):
    packed, width = block.shape
    rows = packed // 2
    units = w_gate.shape[2]
    steps = width // STEP
    part = groups * slots
    pick = jnp.stack([spreader(slots, groups, False), spreader(slots, groups, True)])
    per_slice = steps // 2

    def rows_of(k, order):
        step = k // 2
        return (0, order[k % 2 * 2 + step // per_slice] * per_slice + step % per_slice, 0)

    weights = pl.BlockSpec((1, STEP, units), rows_of)

    def kernel(order_ref, x_ref, pick_ref, wg_ref, wu_ref, act_ref, row_ref, gate_ref, up_ref):
        k = pl.program_id(0)

        @pl.when(k == 0)
        def _():
            gate_ref[...] = jnp.zeros_like(gate_ref)
            up_ref[...] = jnp.zeros_like(up_ref)

        for b in range(rows // part):
            row_ref[b * part : (b + 1) * part, :] = dot(
                pick_ref[0], x_ref[2 * b * part : 2 * (b + 1) * part, :]
            ).astype(BF16)
        x = row_ref[...]
        gate_ref[...] += dot(x, wg_ref[0])
        up_ref[...] += dot(x, wu_ref[0])

        @pl.when(k == 2 * steps - 1)
        def _():
            act_ref[...] = gated(gate_ref[...], up_ref[...])

    return call(
        kernel,
        40,
        order,
        2 * steps,
        [
            pl.BlockSpec((packed, STEP), lambda k, order: (0, k // 2)),
            pl.BlockSpec((1, part, 2 * part), lambda k, order: (k % 2, 0, 0)),
            weights,
            weights,
        ],
        whole((rows, units)),
        jax.ShapeDtypeStruct((rows, units), BF16),
        [pltpu.VMEM((rows, STEP), BF16)] + [pltpu.VMEM((rows, units), F32)] * 2,
        block,
        pick,
        w_gate,
        w_up,
    )


def packed_out(act, slots, groups, order, w_down, down_theirs):
    act_theirs = half_swap(act)
    rows, units = act.shape
    width = down_theirs[0].shape[1]
    per_slice = width // OUT_STEP
    part = groups * slots
    place = jnp.stack([spreader(slots, groups, False).T, spreader(slots, groups, True).T])

    def kernel(order_ref, mine_ref, theirs_ref, place_ref, *refs):
        low_mine, high_mine, low_theirs, high_theirs, out_ref = refs
        low = dot(mine_ref[...], low_mine[0]) + dot(theirs_ref[...], low_theirs[...])
        high = dot(mine_ref[...], high_mine[0]) + dot(theirs_ref[...], high_theirs[...])
        low, high = low.astype(BF16), high.astype(BF16)
        for b in range(rows // part):
            here = slice(b * part, (b + 1) * part)
            both = dot(place_ref[0], low[here]) + dot(place_ref[1], high[here])
            out_ref[2 * b * part : 2 * (b + 1) * part, :] = both.astype(BF16)

    def columns(number):
        return pl.BlockSpec((1, units, OUT_STEP), lambda k, order: (0, 0, order[number] * per_slice + k))

    return call(
        kernel,
        40,
        order,
        per_slice,
        [whole((rows, units)), whole((rows, units)), whole(place.shape), columns(0), columns(1)]
        + [pl.BlockSpec((units, OUT_STEP), lambda k, order: (0, k))] * 2,
        pl.BlockSpec((2 * rows, OUT_STEP), lambda k, order: (0, k)),
        jax.ShapeDtypeStruct((2 * rows, width), BF16),
        [],
        act,
        act_theirs,
        place,
        w_down,
        w_down,
        *down_theirs,
    )


def per_device(
    query_states,
    key_states,
    value_states,
    selected,
    residual,
    out_weight,
    norm_gain,
    w_gate,
    w_up,
    w_down,
    routes,
    route_weights,
):
    count = lax.axis_size("seq")
    exp = lax.axis_index("exp")
    rows, width = residual.shape
    heads = out_weight.shape[0]
    model_width = 4 * width
    group = exp // 2
    side = (exp >= 2).astype(jnp.int32)
    half = jnp.where(jnp.logical_or(exp == 0, exp == 3), 0, 1)
    other = 1 - half

    def ordered(mine, theirs):
        lower = side == 0
        return jnp.concatenate(
            [jnp.where(lower, mine, theirs), jnp.where(lower, theirs, mine)], axis=1
        )

    order = jnp.stack([half, 3 - half, other, 3 - other])
    theirs_order = jnp.stack([other, 3 - other, half, 3 - half])

    down_theirs = [
        half_swap(lax.dynamic_slice_in_dim(w_down[0], theirs_order[n] * width, width, 1))
        for n in range(2)
    ]
    full_out = lax.all_gather(out_weight.reshape(-1, model_width), "seq", axis=0, tiled=True)
    gain = norm_gain[None, :]
    gain_mine = ordered(gain, group_swap(gain))
    gain_theirs = half_swap(gain_mine)
    residual_half = ordered(residual, group_swap(residual))

    experts = 2 * jnp.arange(count, dtype=jnp.int32) + group
    named = routes.T[:, None, :] == experts[None, :, None]
    hits = jnp.any(named, axis=0)
    token_weight = jnp.sum(jnp.where(named, route_weights.T[:, None, :].astype(F32), 0.0), axis=0)
    steps = jnp.arange(rows, dtype=jnp.int32)
    earlier = (steps[:, None] < steps[None, :]).astype(BF16)
    rank = jnp.where(hits, dot(hits.astype(BF16), earlier).astype(jnp.int32), -1)

    def slots(first, number):
        ids = first + jnp.arange(number, dtype=jnp.int32)
        return rank[:, None, :] == ids[None, :, None]

    def picker(mask):
        return mask.astype(BF16).reshape(-1, mask.shape[-1])

    def weigher(mask, high):
        empty = jnp.zeros_like(mask)
        mask = jnp.where(
            high,
            jnp.concatenate([empty, mask], axis=1),
            jnp.concatenate([mask, empty], axis=1),
        )
        return jnp.where(mask, token_weight[:, None, :], 0.0).astype(BF16).reshape(-1, rows)

    first = slots(0, SWAPPED)
    last = slots(SWAPPED, DIRECT)
    empty = jnp.zeros_like(last)
    pick_last = jnp.concatenate(
        [
            picker(jnp.concatenate([last, empty], axis=1)),
            picker(jnp.concatenate([empty, last], axis=1)),
        ],
        axis=1,
    )

    attended = attend(query_states, key_states, value_states, selected, heads)
    attended = regroup(attended, heads, count)
    attended, gain_theirs, residual_half = lax.optimization_barrier(
        (attended, gain_theirs, residual_half)
    )
    total = project_sum(attended, full_out, order, theirs_order, width)
    hidden = (total + residual_half.astype(F32)).astype(BF16).astype(F32)
    gained = (hidden * gain_mine.astype(F32)).astype(BF16)
    gained, down_theirs = lax.optimization_barrier((gained, down_theirs))
    gained_other = half_swap(gained)

    received = spread(dot(picker(first), gained).astype(BF16))
    halves = [(gained, gain_mine), (gained_other, gain_theirs)]
    squares = sum(
        jnp.sum(jnp.square(block.astype(F32) / gain_half.astype(F32)), axis=1, keepdims=True)
        for block, gain_half in halves
    )
    scale = lax.rsqrt(squares / model_width + EPSILON)
    both = jnp.concatenate([(block.astype(F32) * scale).astype(BF16) for block, _ in halves], axis=0)
    rows_out = dot(pick_last, both).astype(BF16)
    rows_out, received = lax.optimization_barrier((rows_out, received))
    received_last = spread(rows_out)

    before = half_units(received, gain_mine, order, w_gate, w_up)
    act = half_units(half_swap(received), gain_theirs, theirs_order, w_gate, w_up, before)
    first_out = packed_out(act, SWAPPED, 128 // SWAPPED, order, w_down, down_theirs)
    first_out, received_last = lax.optimization_barrier((first_out, received_last))
    first_out = spread(first_out)
    act = packed_units(received_last, DIRECT, 96 // DIRECT, order, w_gate, w_up)
    last_out = packed_out(act, DIRECT, 96 // DIRECT, order, w_down, down_theirs)
    last_out, first_out = lax.optimization_barrier((last_out, first_out))
    last_out = spread(last_out)

    def combine(high):
        return dot_rows(weigher(first, high), first_out) + dot_rows(weigher(last, high), last_out)

    give = combine(side == 0).astype(BF16)
    keep = combine(side == 1) + jnp.where(side == 0, hidden[:, :width], hidden[:, width:])
    return (keep + group_swap(give).astype(F32)).astype(BF16)


def solution(mesh):
    return jax.shard_map(
        per_device,
        mesh=mesh,
        in_specs=(
            P("seq", "exp"),
            P("seq", "exp"),
            P("seq", "exp"),
            P(),
            P("seq", "exp"),
            P("exp", "seq", None),
            P("exp"),
            P(("seq", "exp"), None, None),
            P(("seq", "exp"), None, None),
            P(("seq", "exp"), None, None),
            P("seq", None),
            P("seq", None),
        ),
        out_specs=P("seq", "exp"),
        check_vma=False,
    )
```

```python
import math

import jax
import jax.numpy as jnp
from jax import lax
from jax.experimental import pallas as pl
from jax.experimental.pallas import tpu as pltpu
from jax.sharding import PartitionSpec as P

EPSILON = 1e-06
NEGATIVE = -1e30
CAP = 20
DIRECT = 12
SWAPPED = CAP - DIRECT
EARLY = 240
STEP = 1792
OUT_STEP = 896
MIB = 2**20
BF16 = jnp.bfloat16
F32 = jnp.float32


def dot(a, b):
    return jnp.dot(a, b, preferred_element_type=F32)


def dot_rows(a, b):
    return lax.dot_general(a, b, (((0,), (0,)), ((), ())), preferred_element_type=F32)


def half_swap(block):
    return lax.ppermute(block, "exp", [(i, i ^ 1) for i in range(4)])


def group_swap(block):
    return lax.ppermute(block, "exp", [(i, 3 - i) for i in range(4)])


def spread(block):
    return lax.all_to_all(block, "seq", split_axis=0, concat_axis=0, tiled=True)


def fetch_blocks(key_states, value_states, selected):
    count = lax.axis_size("seq")
    rows, width = key_states.shape
    piece = 2 * rows // count
    stacked = jnp.concatenate([key_states, value_states], axis=0)
    pieces = spread(stacked).reshape(count, piece, width)
    previous = lax.ppermute(stacked, "seq", [(i, i + 1) for i in range(count - 1)])
    before = jnp.arange(count, dtype=jnp.int32)[:, None] - 1
    place = jnp.argmax(selected == before, axis=1)
    first = jnp.where(place == 0, selected[:, 1], selected[:, 0])
    second = jnp.where(place == 2, selected[:, 1], selected[:, 2])
    others = jnp.stack([first, second], axis=1)
    wanted = jnp.take(pieces, others.reshape(-1), axis=0).reshape(-1, width)
    fetched = spread(wanted)
    return fetched, previous, others


def attend(query_states, key_states, value_states, selected, heads):
    position = lax.axis_index("seq")
    rows, width = query_states.shape
    head_dim = width // heads
    fetched, previous, others = fetch_blocks(key_states, value_states, selected)
    keys = jnp.concatenate([fetched[: 2 * rows], previous[:rows], key_states], axis=0)
    values = jnp.concatenate([fetched[2 * rows :], previous[rows:], value_states], axis=0)
    keys = keys.reshape(-1, heads, head_dim)
    values = values.reshape(-1, heads, head_dim)
    queries = query_states.reshape(rows, heads, head_dim)
    scores = jnp.einsum("qhd,khd->hqk", queries, keys, preferred_element_type=F32) * (
        1.0 / math.sqrt(head_dim)
    )
    mine = lax.dynamic_slice_in_dim(others, position, 1, 0)[0] < position
    turn = jnp.arange(2 * rows, dtype=jnp.int32) // (2 * rows // lax.axis_size("seq")) % 2
    far = jnp.where(turn == 0, mine[0], mine[1])
    far = jnp.concatenate([far, jnp.broadcast_to(position > 0, (rows,))])
    places = jnp.arange(rows, dtype=jnp.int32)
    causal = places[None, :] <= places[:, None]
    visible = jnp.concatenate(
        [jnp.broadcast_to(far[None, :], (rows, far.shape[0])), causal], axis=1
    )
    scores = jnp.where(visible[None], scores, NEGATIVE)
    peak = jnp.max(scores, axis=2, keepdims=True)
    weights = jnp.exp(scores - peak)
    total = jnp.sum(weights, axis=2, keepdims=True)
    soft_weights = (weights / total).astype(BF16)
    attended = jnp.einsum("hqk,khd->qhd", soft_weights, values, preferred_element_type=F32)
    return attended.astype(BF16).reshape(rows, width)


def regroup(attended, heads, pieces):
    width = attended.shape[1]
    head_dim = width // heads
    piece = head_dim // pieces
    old = jnp.arange(width, dtype=jnp.int32)
    new_of_old = (old % head_dim) // piece * (heads * piece) + old // head_dim * piece + old % piece
    move = (new_of_old[:, None] == jnp.arange(width, dtype=jnp.int32)[None, :]).astype(BF16)
    return dot(attended, move).astype(BF16)


def project_sum(attended, full_out, order, theirs_order, width, behind):
    def product(index):
        columns = lax.dynamic_slice_in_dim(full_out, index * width, width, 1)
        return dot(attended, columns).astype(BF16)

    given = [half_swap(product(theirs_order[n])) for n in range(2)]
    kept = [product(order[n]) for n in range(2)]
    given[0], behind = lax.optimization_barrier((given[0], behind))
    pairs = [(a.astype(F32) + b.astype(F32)).astype(BF16) for a, b in zip(kept, given)]
    total = [pair.astype(F32) + group_swap(pair).astype(F32) for pair in pairs]
    return jnp.concatenate(total, axis=1), behind


def lane_sums(block):
    total = block[:, :128]
    for low in range(128, block.shape[1], 128):
        total = total + block[:, low : low + 128]
    return total


def gated(gate, up):
    return (gate / (1.0 + jnp.exp(-gate)) * up).astype(BF16)


def call(kernel, vmem, order, steps, in_specs, out_specs, out_shape, scratch, *args):
    return pl.pallas_call(
        kernel,
        grid_spec=pltpu.PrefetchScalarGridSpec(
            num_scalar_prefetch=1,
            grid=(steps,),
            in_specs=in_specs,
            out_specs=out_specs,
            scratch_shapes=scratch,
        ),
        out_shape=out_shape,
        compiler_params=pltpu.CompilerParams(
            dimension_semantics=("arbitrary",), vmem_limit_bytes=vmem * MIB
        ),
        cost_estimate=pl.CostEstimate(flops=1000, bytes_accessed=1000, transcendentals=0),
    )(order, *args)


def whole(shape):
    return pl.BlockSpec(shape, lambda k, order: (0,) * len(shape))


def weight_rows(per_slice, units):
    return pl.BlockSpec(
        (1, STEP, units), lambda k, order: (0, order[k // per_slice] * per_slice + k % per_slice, 0)
    )


def half_units(block, gain_half, order, w_gate, w_up, before=None):
    rows, width = block.shape
    units = w_gate.shape[2]
    steps = width // STEP

    def kernel(order_ref, x_ref, gain_ref, wg_ref, wu_ref, *refs):
        k = pl.program_id(0)
        if before is None:
            gate_ref, up_ref, square_ref = refs
        else:
            gate_in, up_in, square_in, act_ref, gate_ref, up_ref, square_ref = refs

        @pl.when(k == 0)
        def _():
            for ref, start in zip(
                (gate_ref, up_ref, square_ref), (None,) * 3 if before is None else refs[:3]
            ):
                ref[...] = jnp.zeros_like(ref) if start is None else start[...]

        x = x_ref[...]
        gate_ref[...] += dot(x, wg_ref[0])
        up_ref[...] += dot(x, wu_ref[0])
        plain = x.astype(F32) * (1.0 / gain_ref[...].astype(F32))
        square_ref[...] += lane_sums(plain * plain)
        if before is not None:

            @pl.when(k == steps - 1)
            def _():
                total = jnp.sum(square_ref[...], axis=1, keepdims=True)
                scale = lax.rsqrt(total / (2 * width) + EPSILON)
                act_ref[...] = gated(gate_ref[...] * scale, up_ref[...] * scale)

    per_slice = steps // 2
    in_specs = [
        pl.BlockSpec((rows, STEP), lambda k, order: (0, k)),
        pl.BlockSpec((1, STEP), lambda k, order: (0, k)),
        weight_rows(per_slice, units),
        weight_rows(per_slice, units),
    ]
    sums = [(rows, units), (rows, units), (rows, 128)]
    args = [block, gain_half, w_gate, w_up]
    if before is None:
        return call(
            kernel,
            20,
            order,
            steps,
            in_specs,
            [whole(shape) for shape in sums],
            [jax.ShapeDtypeStruct(shape, F32) for shape in sums],
            [],
            *args,
        )
    return call(
        kernel,
        20,
        order,
        steps,
        in_specs + [whole(shape) for shape in sums],
        whole((rows, units)),
        jax.ShapeDtypeStruct((rows, units), BF16),
        [pltpu.VMEM(shape, F32) for shape in sums],
        *args,
        *before,
    )


def unpacker(slots, groups):
    row = jnp.arange(groups * slots, dtype=jnp.int32)
    low = row // slots * 2 * slots + row % slots
    place = jnp.concatenate([low, low + slots])
    return (place[:, None] == jnp.arange(groups * 2 * slots, dtype=jnp.int32)[None, :]).astype(BF16)


def packed_units(block, slots, groups, order, w_gate, w_up):
    packed, width = block.shape
    rows = packed // 2
    units = w_gate.shape[2]
    steps = width // STEP
    part = groups * slots
    pick = unpacker(slots, groups)
    per_slice = steps // 2

    def rows_of(k, order):
        step = k // 2
        return (0, order[k % 2 * 2 + step // per_slice] * per_slice + step % per_slice, 0)

    weights = pl.BlockSpec((1, STEP, units), rows_of)

    def kernel(order_ref, x_ref, pick_ref, wg_ref, wu_ref, act_ref, row_ref, gate_ref, up_ref):
        k = pl.program_id(0)

        @pl.when(k == 0)
        def _():
            gate_ref[...] = jnp.zeros_like(gate_ref)
            up_ref[...] = jnp.zeros_like(up_ref)

        @pl.when(k % 2 == 0)
        def _():
            for b in range(rows // part):
                both = dot(pick_ref[...], x_ref[2 * b * part : 2 * (b + 1) * part, :]).astype(BF16)
                row_ref[0, b * part : (b + 1) * part, :] = both[:part]
                row_ref[1, b * part : (b + 1) * part, :] = both[part:]

        x = row_ref[k % 2]
        gate_ref[...] += dot(x, wg_ref[0])
        up_ref[...] += dot(x, wu_ref[0])

        @pl.when(k == 2 * steps - 1)
        def _():
            act_ref[...] = gated(gate_ref[...], up_ref[...])

    return call(
        kernel,
        40,
        order,
        2 * steps,
        [
            pl.BlockSpec((packed, STEP), lambda k, order: (0, k // 2)),
            whole(pick.shape),
            weights,
            weights,
        ],
        whole((rows, units)),
        jax.ShapeDtypeStruct((rows, units), BF16),
        [pltpu.VMEM((2, rows, STEP), BF16)] + [pltpu.VMEM((rows, units), F32)] * 2,
        block,
        pick,
        w_gate,
        w_up,
    )


def packed_out(act, slots, groups, order, w_down, down_theirs):
    act_theirs = half_swap(act)
    rows, units = act.shape
    width = down_theirs[0].shape[1]
    per_slice = width // OUT_STEP
    part = groups * slots
    place = unpacker(slots, groups).T

    def kernel(order_ref, mine_ref, theirs_ref, place_ref, *refs):
        low_mine, high_mine, low_theirs, high_theirs, out_ref = refs
        low = dot(mine_ref[...], low_mine[0]) + dot(theirs_ref[...], low_theirs[...])
        high = dot(mine_ref[...], high_mine[0]) + dot(theirs_ref[...], high_theirs[...])
        low, high = low.astype(BF16), high.astype(BF16)
        for b in range(rows // part):
            here = slice(b * part, (b + 1) * part)
            both = dot(place_ref[...], jnp.concatenate([low[here], high[here]], axis=0))
            out_ref[2 * b * part : 2 * (b + 1) * part, :] = both.astype(BF16)

    def columns(number):
        return pl.BlockSpec((1, units, OUT_STEP), lambda k, order: (0, 0, order[number] * per_slice + k))

    return call(
        kernel,
        40,
        order,
        per_slice,
        [whole((rows, units)), whole((rows, units)), whole(place.shape), columns(0), columns(1)]
        + [pl.BlockSpec((units, OUT_STEP), lambda k, order: (0, k))] * 2,
        pl.BlockSpec((2 * rows, OUT_STEP), lambda k, order: (0, k)),
        jax.ShapeDtypeStruct((2 * rows, width), BF16),
        [],
        act,
        act_theirs,
        place,
        w_down,
        w_down,
        *down_theirs,
    )


def per_device(
    query_states,
    key_states,
    value_states,
    selected,
    residual,
    out_weight,
    norm_gain,
    w_gate,
    w_up,
    w_down,
    routes,
    route_weights,
):
    count = lax.axis_size("seq")
    exp = lax.axis_index("exp")
    rows, width = residual.shape
    heads = out_weight.shape[0]
    model_width = 4 * width
    group = exp // 2
    side = (exp >= 2).astype(jnp.int32)
    half = jnp.where(jnp.logical_or(exp == 0, exp == 3), 0, 1)
    other = 1 - half

    def ordered(mine, theirs):
        lower = side == 0
        return jnp.concatenate(
            [jnp.where(lower, mine, theirs), jnp.where(lower, theirs, mine)], axis=1
        )

    order = jnp.stack([half, 3 - half, other, 3 - other])
    theirs_order = jnp.stack([other, 3 - other, half, 3 - half])

    full_out = lax.all_gather(out_weight.reshape(-1, model_width), "seq", axis=0, tiled=True)
    gain = norm_gain[None, :]
    gain_mine = ordered(gain, group_swap(gain))
    gain_theirs = half_swap(gain_mine)
    residual_half = ordered(residual, group_swap(residual))

    down_given = [
        lax.dynamic_slice_in_dim(w_down[0], theirs_order[n] * width, width, 1) for n in range(2)
    ]
    down_given, gain_theirs = lax.optimization_barrier((down_given, gain_theirs))
    early = [half_swap(down_given[0]), half_swap(down_given[1][:EARLY])]

    experts = 2 * jnp.arange(count, dtype=jnp.int32) + group
    named = routes.T[:, None, :] == experts[None, :, None]
    hits = jnp.any(named, axis=0)
    token_weight = jnp.sum(jnp.where(named, route_weights.T[:, None, :].astype(F32), 0.0), axis=0)
    steps = jnp.arange(rows, dtype=jnp.int32)
    earlier = (steps[:, None] < steps[None, :]).astype(BF16)
    rank = jnp.where(hits, dot(hits.astype(BF16), earlier).astype(jnp.int32), -1)

    def slots(first, number):
        ids = first + jnp.arange(number, dtype=jnp.int32)
        return rank[:, None, :] == ids[None, :, None]

    def picker(mask):
        return mask.astype(BF16).reshape(-1, mask.shape[-1])

    def weigher(mask, high):
        empty = jnp.zeros_like(mask)
        mask = jnp.where(
            high,
            jnp.concatenate([empty, mask], axis=1),
            jnp.concatenate([mask, empty], axis=1),
        )
        return jnp.where(mask, token_weight[:, None, :], 0.0).astype(BF16).reshape(-1, rows)

    first = slots(0, SWAPPED)
    last = slots(SWAPPED, DIRECT)
    empty = jnp.zeros_like(last)
    pick_last = jnp.concatenate(
        [
            picker(jnp.concatenate([last, empty], axis=1)),
            picker(jnp.concatenate([empty, last], axis=1)),
        ],
        axis=1,
    )

    attended = attend(query_states, key_states, value_states, selected, heads)
    attended = regroup(attended, heads, count)
    attended, early, residual_half = lax.optimization_barrier((attended, early, residual_half))
    total, late = project_sum(
        attended, full_out, order, theirs_order, width, down_given[1][EARLY:]
    )
    late = half_swap(late)
    hidden = (total + residual_half.astype(F32)).astype(BF16).astype(F32)
    gained = (hidden * gain_mine.astype(F32)).astype(BF16)
    gained_other = half_swap(gained)

    received = spread(dot(picker(first), gained).astype(BF16))
    halves = [(gained, gain_mine), (gained_other, gain_theirs)]
    squares = sum(
        jnp.sum(jnp.square(block.astype(F32) / gain_half.astype(F32)), axis=1, keepdims=True)
        for block, gain_half in halves
    )
    scale = lax.rsqrt(squares / model_width + EPSILON)
    both = jnp.concatenate([(block.astype(F32) * scale).astype(BF16) for block, _ in halves], axis=0)
    rows_out = dot(pick_last, both).astype(BF16)
    rows_out, received, late = lax.optimization_barrier((rows_out, received, late))
    down_theirs = [early[0], jnp.concatenate([early[1], late], axis=0)]
    received_last = spread(rows_out)

    before = half_units(received, gain_mine, order, w_gate, w_up)
    act = half_units(half_swap(received), gain_theirs, theirs_order, w_gate, w_up, before)
    first_out = packed_out(act, SWAPPED, 128 // SWAPPED, order, w_down, down_theirs)
    first_out, received_last = lax.optimization_barrier((first_out, received_last))
    first_out = spread(first_out)
    act = packed_units(received_last, DIRECT, 96 // DIRECT, order, w_gate, w_up)
    last_out = packed_out(act, DIRECT, 96 // DIRECT, order, w_down, down_theirs)
    last_out, first_out = lax.optimization_barrier((last_out, first_out))
    last_out = spread(last_out)

    high = side == 0
    give = dot_rows(weigher(first, high), first_out)
    keep = dot_rows(weigher(first, ~high), first_out)
    keep = keep + jnp.where(high, hidden[:, :width], hidden[:, width:])
    give_last, keep_last = weigher(last, high), weigher(last, ~high)
    last_out, give, keep, give_last, keep_last = lax.optimization_barrier(
        (last_out, give, keep, give_last, keep_last)
    )
    give = group_swap((give + dot_rows(give_last, last_out)).astype(BF16))
    keep = keep + dot_rows(keep_last, last_out)
    return (keep + give.astype(F32)).astype(BF16)


def solution(mesh):
    return jax.shard_map(
        per_device,
        mesh=mesh,
        in_specs=(
            P("seq", "exp"),
            P("seq", "exp"),
            P("seq", "exp"),
            P(),
            P("seq", "exp"),
            P("exp", "seq", None),
            P("exp"),
            P(("seq", "exp"), None, None),
            P(("seq", "exp"), None, None),
            P(("seq", "exp"), None, None),
            P("seq", None),
            P("seq", None),
        ),
        out_specs=P("seq", "exp"),
        check_vma=False,
    )
```

```python
import math

import jax
import jax.numpy as jnp
from jax import lax
from jax.experimental import pallas as pl
from jax.experimental.pallas import tpu as pltpu
from jax.sharding import PartitionSpec as P

EPSILON = 1e-06
NEGATIVE = -1e30
CAP = 20
DIRECT = 12
SWAPPED = CAP - DIRECT
EARLY = 208
MIDDLE = 320
STEP = 1792
OUT_STEP = 896
MIB = 2**20
BF16 = jnp.bfloat16
F32 = jnp.float32


def dot(a, b):
    return jnp.dot(a, b, preferred_element_type=F32)


def dot_rows(a, b):
    return lax.dot_general(a, b, (((0,), (0,)), ((), ())), preferred_element_type=F32)


def half_swap(block):
    return lax.ppermute(block, "exp", [(i, i ^ 1) for i in range(4)])


def group_swap(block):
    return lax.ppermute(block, "exp", [(i, 3 - i) for i in range(4)])


def spread(block):
    return lax.all_to_all(block, "seq", split_axis=0, concat_axis=0, tiled=True)


def fetch_blocks(key_states, value_states, selected):
    count = lax.axis_size("seq")
    rows, width = key_states.shape
    piece = 2 * rows // count
    stacked = jnp.concatenate([key_states, value_states], axis=0)
    pieces = spread(stacked).reshape(count, piece, width)
    previous = lax.ppermute(stacked, "seq", [(i, i + 1) for i in range(count - 1)])
    before = jnp.arange(count, dtype=jnp.int32)[:, None] - 1
    place = jnp.argmax(selected == before, axis=1)
    first = jnp.where(place == 0, selected[:, 1], selected[:, 0])
    second = jnp.where(place == 2, selected[:, 1], selected[:, 2])
    others = jnp.stack([first, second], axis=1)
    wanted = jnp.take(pieces, others.reshape(-1), axis=0).reshape(-1, width)
    fetched = spread(wanted)
    return fetched, previous, others


def attend(query_states, key_states, value_states, selected, heads):
    position = lax.axis_index("seq")
    rows, width = query_states.shape
    head_dim = width // heads
    fetched, previous, others = fetch_blocks(key_states, value_states, selected)
    keys = jnp.concatenate([fetched[: 2 * rows], previous[:rows], key_states], axis=0)
    values = jnp.concatenate([fetched[2 * rows :], previous[rows:], value_states], axis=0)
    keys = keys.reshape(-1, heads, head_dim)
    values = values.reshape(-1, heads, head_dim)
    queries = query_states.reshape(rows, heads, head_dim)
    scores = jnp.einsum("qhd,khd->hqk", queries, keys, preferred_element_type=F32) * (
        1.0 / math.sqrt(head_dim)
    )
    mine = lax.dynamic_slice_in_dim(others, position, 1, 0)[0] < position
    turn = jnp.arange(2 * rows, dtype=jnp.int32) // (2 * rows // lax.axis_size("seq")) % 2
    far = jnp.where(turn == 0, mine[0], mine[1])
    far = jnp.concatenate([far, jnp.broadcast_to(position > 0, (rows,))])
    places = jnp.arange(rows, dtype=jnp.int32)
    causal = places[None, :] <= places[:, None]
    visible = jnp.concatenate(
        [jnp.broadcast_to(far[None, :], (rows, far.shape[0])), causal], axis=1
    )
    scores = jnp.where(visible[None], scores, NEGATIVE)
    peak = jnp.max(scores, axis=2, keepdims=True)
    weights = jnp.exp(scores - peak)
    total = jnp.sum(weights, axis=2, keepdims=True)
    soft_weights = (weights / total).astype(BF16)
    attended = jnp.einsum("hqk,khd->qhd", soft_weights, values, preferred_element_type=F32)
    return attended.astype(BF16).reshape(rows, width)


def regroup(attended, heads, pieces):
    width = attended.shape[1]
    head_dim = width // heads
    piece = head_dim // pieces
    old = jnp.arange(width, dtype=jnp.int32)
    new_of_old = (old % head_dim) // piece * (heads * piece) + old // head_dim * piece + old % piece
    move = (new_of_old[:, None] == jnp.arange(width, dtype=jnp.int32)[None, :]).astype(BF16)
    return dot(attended, move).astype(BF16)


def project_sum(attended, full_out, order, theirs_order, width, behind):
    def product(index):
        columns = lax.dynamic_slice_in_dim(full_out, index * width, width, 1)
        return dot(attended, columns).astype(BF16)

    given = [half_swap(product(theirs_order[n])) for n in range(2)]
    kept = [product(order[n]) for n in range(2)]
    for n in range(2):
        given[n], kept[n] = lax.optimization_barrier((given[n], kept[n]))
    given[0], behind = lax.optimization_barrier((given[0], behind))
    pairs = [(a.astype(F32) + b.astype(F32)).astype(BF16) for a, b in zip(kept, given)]
    total = [pair.astype(F32) + group_swap(pair).astype(F32) for pair in pairs]
    return jnp.concatenate(total, axis=1), behind


def lane_sums(block):
    total = block[:, :128]
    for low in range(128, block.shape[1], 128):
        total = total + block[:, low : low + 128]
    return total


def gated(gate, up):
    return (gate / (1.0 + jnp.exp(-gate)) * up).astype(BF16)


def call(kernel, vmem, order, steps, in_specs, out_specs, out_shape, scratch, *args):
    return pl.pallas_call(
        kernel,
        grid_spec=pltpu.PrefetchScalarGridSpec(
            num_scalar_prefetch=1,
            grid=(steps,),
            in_specs=in_specs,
            out_specs=out_specs,
            scratch_shapes=scratch,
        ),
        out_shape=out_shape,
        compiler_params=pltpu.CompilerParams(
            dimension_semantics=("arbitrary",), vmem_limit_bytes=vmem * MIB
        ),
        cost_estimate=pl.CostEstimate(flops=1000, bytes_accessed=1000, transcendentals=0),
    )(order, *args)


def whole(shape):
    return pl.BlockSpec(shape, lambda k, order: (0,) * len(shape))


def weight_rows(per_slice, units):
    return pl.BlockSpec(
        (1, STEP, units), lambda k, order: (0, order[k // per_slice] * per_slice + k % per_slice, 0)
    )


def half_units(block, gain_half, order, w_gate, w_up, before=None):
    rows, width = block.shape
    units = w_gate.shape[2]
    steps = width // STEP

    def kernel(order_ref, x_ref, gain_ref, wg_ref, wu_ref, *refs):
        k = pl.program_id(0)
        if before is None:
            gate_ref, up_ref, square_ref = refs
        else:
            gate_in, up_in, square_in, act_ref, gate_ref, up_ref, square_ref = refs

        @pl.when(k == 0)
        def _():
            for ref, start in zip(
                (gate_ref, up_ref, square_ref), (None,) * 3 if before is None else refs[:3]
            ):
                ref[...] = jnp.zeros_like(ref) if start is None else start[...]

        x = x_ref[...]
        gate_ref[...] += dot(x, wg_ref[0])
        up_ref[...] += dot(x, wu_ref[0])
        plain = x.astype(F32) * (1.0 / gain_ref[...].astype(F32))
        square_ref[...] += lane_sums(plain * plain)
        if before is not None:

            @pl.when(k == steps - 1)
            def _():
                total = jnp.sum(square_ref[...], axis=1, keepdims=True)
                scale = lax.rsqrt(total / (2 * width) + EPSILON)
                act_ref[...] = gated(gate_ref[...] * scale, up_ref[...] * scale)

    per_slice = steps // 2
    in_specs = [
        pl.BlockSpec((rows, STEP), lambda k, order: (0, k)),
        pl.BlockSpec((1, STEP), lambda k, order: (0, k)),
        weight_rows(per_slice, units),
        weight_rows(per_slice, units),
    ]
    sums = [(rows, units), (rows, units), (rows, 128)]
    args = [block, gain_half, w_gate, w_up]
    if before is None:
        return call(
            kernel,
            20,
            order,
            steps,
            in_specs,
            [whole(shape) for shape in sums],
            [jax.ShapeDtypeStruct(shape, F32) for shape in sums],
            [],
            *args,
        )
    return call(
        kernel,
        20,
        order,
        steps,
        in_specs + [whole(shape) for shape in sums],
        whole((rows, units)),
        jax.ShapeDtypeStruct((rows, units), BF16),
        [pltpu.VMEM(shape, F32) for shape in sums],
        *args,
        *before,
    )


def unpacker(slots, groups):
    row = jnp.arange(groups * slots, dtype=jnp.int32)
    low = row // slots * 2 * slots + row % slots
    place = jnp.concatenate([low, low + slots])
    return (place[:, None] == jnp.arange(groups * 2 * slots, dtype=jnp.int32)[None, :]).astype(BF16)


def packed_units(block, slots, groups, order, w_gate, w_up):
    packed, width = block.shape
    rows = packed // 2
    units = w_gate.shape[2]
    steps = width // STEP
    part = groups * slots
    pick = unpacker(slots, groups)
    per_slice = steps // 2

    def rows_of(k, order):
        step = k // 2
        return (0, order[k % 2 * 2 + step // per_slice] * per_slice + step % per_slice, 0)

    weights = pl.BlockSpec((1, STEP, units), rows_of)

    def kernel(order_ref, x_ref, pick_ref, wg_ref, wu_ref, act_ref, row_ref, gate_ref, up_ref):
        k = pl.program_id(0)

        @pl.when(k == 0)
        def _():
            gate_ref[...] = jnp.zeros_like(gate_ref)
            up_ref[...] = jnp.zeros_like(up_ref)

        @pl.when(k % 2 == 0)
        def _():
            for b in range(rows // part):
                both = dot(pick_ref[...], x_ref[2 * b * part : 2 * (b + 1) * part, :]).astype(BF16)
                row_ref[0, b * part : (b + 1) * part, :] = both[:part]
                row_ref[1, b * part : (b + 1) * part, :] = both[part:]

        x = row_ref[k % 2]
        gate_ref[...] += dot(x, wg_ref[0])
        up_ref[...] += dot(x, wu_ref[0])

        @pl.when(k == 2 * steps - 1)
        def _():
            act_ref[...] = gated(gate_ref[...], up_ref[...])

    return call(
        kernel,
        40,
        order,
        2 * steps,
        [
            pl.BlockSpec((packed, STEP), lambda k, order: (0, k // 2)),
            whole(pick.shape),
            weights,
            weights,
        ],
        whole((rows, units)),
        jax.ShapeDtypeStruct((rows, units), BF16),
        [pltpu.VMEM((2, rows, STEP), BF16)] + [pltpu.VMEM((rows, units), F32)] * 2,
        block,
        pick,
        w_gate,
        w_up,
    )


def packed_out(act, slots, groups, order, w_down, down_theirs):
    act_theirs = half_swap(act)
    rows, units = act.shape
    width = down_theirs[0].shape[1]
    per_slice = width // OUT_STEP
    part = groups * slots
    place = unpacker(slots, groups).T

    def kernel(order_ref, mine_ref, theirs_ref, place_ref, *refs):
        low_mine, high_mine, low_theirs, high_theirs, out_ref = refs
        low = dot(mine_ref[...], low_mine[0]) + dot(theirs_ref[...], low_theirs[...])
        high = dot(mine_ref[...], high_mine[0]) + dot(theirs_ref[...], high_theirs[...])
        low, high = low.astype(BF16), high.astype(BF16)
        for b in range(rows // part):
            here = slice(b * part, (b + 1) * part)
            both = dot(place_ref[...], jnp.concatenate([low[here], high[here]], axis=0))
            out_ref[2 * b * part : 2 * (b + 1) * part, :] = both.astype(BF16)

    def columns(number):
        return pl.BlockSpec((1, units, OUT_STEP), lambda k, order: (0, 0, order[number] * per_slice + k))

    return call(
        kernel,
        40,
        order,
        per_slice,
        [whole((rows, units)), whole((rows, units)), whole(place.shape), columns(0), columns(1)]
        + [pl.BlockSpec((units, OUT_STEP), lambda k, order: (0, k))] * 2,
        pl.BlockSpec((2 * rows, OUT_STEP), lambda k, order: (0, k)),
        jax.ShapeDtypeStruct((2 * rows, width), BF16),
        [],
        act,
        act_theirs,
        place,
        w_down,
        w_down,
        *down_theirs,
    )


def per_device(
    query_states,
    key_states,
    value_states,
    selected,
    residual,
    out_weight,
    norm_gain,
    w_gate,
    w_up,
    w_down,
    routes,
    route_weights,
):
    count = lax.axis_size("seq")
    exp = lax.axis_index("exp")
    rows, width = residual.shape
    heads = out_weight.shape[0]
    model_width = 4 * width
    group = exp // 2
    side = (exp >= 2).astype(jnp.int32)
    half = jnp.where(jnp.logical_or(exp == 0, exp == 3), 0, 1)
    other = 1 - half

    def ordered(mine, theirs):
        lower = side == 0
        return jnp.concatenate(
            [jnp.where(lower, mine, theirs), jnp.where(lower, theirs, mine)], axis=1
        )

    order = jnp.stack([half, 3 - half, other, 3 - other])
    theirs_order = jnp.stack([other, 3 - other, half, 3 - half])

    full_out = lax.all_gather(out_weight.reshape(-1, model_width), "seq", axis=0, tiled=True)
    gain = norm_gain[None, :]
    gain_mine = ordered(gain, group_swap(gain))
    gain_theirs = half_swap(gain_mine)
    residual_half = ordered(residual, group_swap(residual))

    down_given = [
        lax.dynamic_slice_in_dim(w_down[0], theirs_order[n] * width, width, 1) for n in range(2)
    ]
    down_given, gain_theirs = lax.optimization_barrier((down_given, gain_theirs))
    early = [half_swap(down_given[0]), half_swap(down_given[1][:EARLY])]

    experts = 2 * jnp.arange(count, dtype=jnp.int32) + group
    named = routes.T[:, None, :] == experts[None, :, None]
    hits = jnp.any(named, axis=0)
    token_weight = jnp.sum(jnp.where(named, route_weights.T[:, None, :].astype(F32), 0.0), axis=0)
    steps = jnp.arange(rows, dtype=jnp.int32)
    earlier = (steps[:, None] < steps[None, :]).astype(BF16)
    rank = jnp.where(hits, dot(hits.astype(BF16), earlier).astype(jnp.int32), -1)

    def slots(first, number):
        ids = first + jnp.arange(number, dtype=jnp.int32)
        return rank[:, None, :] == ids[None, :, None]

    def picker(mask):
        return mask.astype(BF16).reshape(-1, mask.shape[-1])

    def weigher(mask, high):
        empty = jnp.zeros_like(mask)
        mask = jnp.where(
            high,
            jnp.concatenate([empty, mask], axis=1),
            jnp.concatenate([mask, empty], axis=1),
        )
        return jnp.where(mask, token_weight[:, None, :], 0.0).astype(BF16).reshape(-1, rows)

    first = slots(0, SWAPPED)
    last = slots(SWAPPED, DIRECT)
    empty = jnp.zeros_like(last)
    pick_last = jnp.concatenate(
        [
            picker(jnp.concatenate([last, empty], axis=1)),
            picker(jnp.concatenate([empty, last], axis=1)),
        ],
        axis=1,
    )

    attended = attend(query_states, key_states, value_states, selected, heads)
    attended = regroup(attended, heads, count)
    late = [down_given[1][EARLY:MIDDLE], down_given[1][MIDDLE:]]
    attended, early, late, residual_half = lax.optimization_barrier(
        (attended, early, late, residual_half)
    )
    total, late = project_sum(attended, full_out, order, theirs_order, width, late)
    late = [half_swap(block) for block in late]
    hidden = (total + residual_half.astype(F32)).astype(BF16).astype(F32)
    gained = (hidden * gain_mine.astype(F32)).astype(BF16)
    gained, late[0] = lax.optimization_barrier((gained, late[0]))
    gained_other = half_swap(gained)

    received = spread(dot(picker(first), gained).astype(BF16))
    halves = [(gained, gain_mine), (gained_other, gain_theirs)]
    squares = sum(
        jnp.sum(jnp.square(block.astype(F32) / gain_half.astype(F32)), axis=1, keepdims=True)
        for block, gain_half in halves
    )
    scale = lax.rsqrt(squares / model_width + EPSILON)
    both = jnp.concatenate([(block.astype(F32) * scale).astype(BF16) for block, _ in halves], axis=0)
    rows_out = dot(pick_last, both).astype(BF16)
    rows_out, received, late[1] = lax.optimization_barrier((rows_out, received, late[1]))
    down_theirs = [early[0], jnp.concatenate([early[1], *late], axis=0)]
    received_last = spread(rows_out)

    before = half_units(received, gain_mine, order, w_gate, w_up)
    act = half_units(half_swap(received), gain_theirs, theirs_order, w_gate, w_up, before)
    first_out = packed_out(act, SWAPPED, 128 // SWAPPED, order, w_down, down_theirs)
    first_out, received_last = lax.optimization_barrier((first_out, received_last))
    first_out = spread(first_out)
    act = packed_units(received_last, DIRECT, 96 // DIRECT, order, w_gate, w_up)
    last_out = packed_out(act, DIRECT, 96 // DIRECT, order, w_down, down_theirs)
    last_out, first_out = lax.optimization_barrier((last_out, first_out))
    last_out = spread(last_out)

    high = side == 0
    give = dot_rows(weigher(first, high), first_out)
    keep = dot_rows(weigher(first, ~high), first_out)
    keep = keep + jnp.where(high, hidden[:, :width], hidden[:, width:])
    give_last, keep_last = weigher(last, high), weigher(last, ~high)
    last_out, give, keep, give_last, keep_last = lax.optimization_barrier(
        (last_out, give, keep, give_last, keep_last)
    )
    give = group_swap((give + dot_rows(give_last, last_out)).astype(BF16))
    keep = keep + dot_rows(keep_last, last_out)
    return (keep + give.astype(F32)).astype(BF16)


def solution(mesh):
    return jax.shard_map(
        per_device,
        mesh=mesh,
        in_specs=(
            P("seq", "exp"),
            P("seq", "exp"),
            P("seq", "exp"),
            P(),
            P("seq", "exp"),
            P("exp", "seq", None),
            P("exp"),
            P(("seq", "exp"), None, None),
            P(("seq", "exp"), None, None),
            P(("seq", "exp"), None, None),
            P("seq", None),
            P("seq", None),
        ),
        out_specs=P("seq", "exp"),
        check_vma=False,
    )
```

```python
import math

import jax
import jax.numpy as jnp
from jax import lax
from jax.experimental import pallas as pl
from jax.experimental.pallas import tpu as pltpu
from jax.sharding import PartitionSpec as P

EPSILON = 1e-06
NEGATIVE = -1e30
CAP = 20
DIRECT = 12
SWAPPED = CAP - DIRECT
EARLY = 208
MIDDLE = 320
STEP = 1792
OUT_STEP = 896
MIB = 2**20
BF16 = jnp.bfloat16
F32 = jnp.float32


def dot(a, b):
    return jnp.dot(a, b, preferred_element_type=F32)


def dot_rows(a, b):
    return lax.dot_general(a, b, (((0,), (0,)), ((), ())), preferred_element_type=F32)


def half_swap(block):
    return lax.ppermute(block, "exp", [(i, i ^ 1) for i in range(4)])


def group_swap(block):
    return lax.ppermute(block, "exp", [(i, 3 - i) for i in range(4)])


def spread(block):
    return lax.all_to_all(block, "seq", split_axis=0, concat_axis=0, tiled=True)


def fetch_blocks(key_states, value_states, selected):
    count = lax.axis_size("seq")
    rows, width = key_states.shape
    piece = 2 * rows // count
    stacked = jnp.concatenate([key_states, value_states], axis=0)
    pieces = spread(stacked).reshape(count, piece, width)
    previous = lax.ppermute(stacked, "seq", [(i, i + 1) for i in range(count - 1)])
    before = jnp.arange(count, dtype=jnp.int32)[:, None] - 1
    place = jnp.argmax(selected == before, axis=1)
    first = jnp.where(place == 0, selected[:, 1], selected[:, 0])
    second = jnp.where(place == 2, selected[:, 1], selected[:, 2])
    others = jnp.stack([first, second], axis=1)
    wanted = jnp.take(pieces, others.reshape(-1), axis=0).reshape(-1, width)
    fetched = spread(wanted)
    return fetched, previous, others


def attend(query_states, key_states, value_states, selected, heads):
    position = lax.axis_index("seq")
    rows, width = query_states.shape
    head_dim = width // heads
    fetched, previous, others = fetch_blocks(key_states, value_states, selected)
    keys = jnp.concatenate([fetched[: 2 * rows], previous[:rows], key_states], axis=0)
    values = jnp.concatenate([fetched[2 * rows :], previous[rows:], value_states], axis=0)
    keys = keys.reshape(-1, heads, head_dim)
    values = values.reshape(-1, heads, head_dim)
    queries = query_states.reshape(rows, heads, head_dim)
    scores = jnp.einsum("qhd,khd->hqk", queries, keys, preferred_element_type=F32) * (
        1.0 / math.sqrt(head_dim)
    )
    mine = lax.dynamic_slice_in_dim(others, position, 1, 0)[0] < position
    turn = jnp.arange(2 * rows, dtype=jnp.int32) // (2 * rows // lax.axis_size("seq")) % 2
    far = jnp.where(turn == 0, mine[0], mine[1])
    far = jnp.concatenate([far, jnp.broadcast_to(position > 0, (rows,))])
    places = jnp.arange(rows, dtype=jnp.int32)
    causal = places[None, :] <= places[:, None]
    visible = jnp.concatenate(
        [jnp.broadcast_to(far[None, :], (rows, far.shape[0])), causal], axis=1
    )
    scores = jnp.where(visible[None], scores, NEGATIVE)
    peak = jnp.max(scores, axis=2, keepdims=True)
    weights = jnp.exp(scores - peak)
    total = jnp.sum(weights, axis=2, keepdims=True)
    soft_weights = (weights / total).astype(BF16)
    attended = jnp.einsum("hqk,khd->qhd", soft_weights, values, preferred_element_type=F32)
    return attended.astype(BF16).reshape(rows, width)


def regroup(attended, heads, pieces):
    width = attended.shape[1]
    head_dim = width // heads
    piece = head_dim // pieces
    old = jnp.arange(width, dtype=jnp.int32)
    new_of_old = (old % head_dim) // piece * (heads * piece) + old // head_dim * piece + old % piece
    move = (new_of_old[:, None] == jnp.arange(width, dtype=jnp.int32)[None, :]).astype(BF16)
    return dot(attended, move).astype(BF16)


def project_sum(attended, full_out, order, theirs_order, width, behind):
    def product(index):
        columns = lax.dynamic_slice_in_dim(full_out, index * width, width, 1)
        return dot(attended, columns).astype(BF16)

    given = [half_swap(product(theirs_order[n])) for n in range(2)]
    kept = [product(order[n]) for n in range(2)]
    for n in range(2):
        given[n], kept[n] = lax.optimization_barrier((given[n], kept[n]))
    given[0], behind = lax.optimization_barrier((given[0], behind))
    pairs = [(a.astype(F32) + b.astype(F32)).astype(BF16) for a, b in zip(kept, given)]
    total = [pair.astype(F32) + group_swap(pair).astype(F32) for pair in pairs]
    return jnp.concatenate(total, axis=1), behind


def lane_sums(block):
    total = block[:, :128]
    for low in range(128, block.shape[1], 128):
        total = total + block[:, low : low + 128]
    return total


def gated(gate, up):
    return (gate / (1.0 + jnp.exp(-gate)) * up).astype(BF16)


def call(kernel, vmem, order, steps, in_specs, out_specs, out_shape, scratch, *args):
    return pl.pallas_call(
        kernel,
        grid_spec=pltpu.PrefetchScalarGridSpec(
            num_scalar_prefetch=1,
            grid=(steps,),
            in_specs=in_specs,
            out_specs=out_specs,
            scratch_shapes=scratch,
        ),
        out_shape=out_shape,
        compiler_params=pltpu.CompilerParams(
            dimension_semantics=("arbitrary",), vmem_limit_bytes=vmem * MIB
        ),
        cost_estimate=pl.CostEstimate(flops=1000, bytes_accessed=1000, transcendentals=0),
    )(order, *args)


def whole(shape):
    return pl.BlockSpec(shape, lambda k, order: (0,) * len(shape))


def weight_rows(per_slice, units):
    return pl.BlockSpec(
        (1, STEP, units), lambda k, order: (0, order[k // per_slice] * per_slice + k % per_slice, 0)
    )


def half_units(block, gain_half, order, w_gate, w_up, before=None):
    rows, width = block.shape
    units = w_gate.shape[2]
    steps = width // STEP

    def kernel(order_ref, x_ref, gain_ref, wg_ref, wu_ref, *refs):
        k = pl.program_id(0)
        if before is None:
            gate_ref, up_ref, square_ref = refs
        else:
            gate_in, up_in, square_in, act_ref, gate_ref, up_ref, square_ref = refs

        @pl.when(k == 0)
        def _():
            for ref, start in zip(
                (gate_ref, up_ref, square_ref), (None,) * 3 if before is None else refs[:3]
            ):
                ref[...] = jnp.zeros_like(ref) if start is None else start[...]

        x = x_ref[...]
        gate_ref[...] += dot(x, wg_ref[0])
        up_ref[...] += dot(x, wu_ref[0])
        plain = x.astype(F32) * (1.0 / gain_ref[...].astype(F32))
        square_ref[...] += lane_sums(plain * plain)
        if before is not None:

            @pl.when(k == steps - 1)
            def _():
                total = jnp.sum(square_ref[...], axis=1, keepdims=True)
                scale = lax.rsqrt(total / (2 * width) + EPSILON)
                act_ref[...] = gated(gate_ref[...] * scale, up_ref[...] * scale)

    per_slice = steps // 2
    in_specs = [
        pl.BlockSpec((rows, STEP), lambda k, order: (0, k)),
        pl.BlockSpec((1, STEP), lambda k, order: (0, k)),
        weight_rows(per_slice, units),
        weight_rows(per_slice, units),
    ]
    sums = [(rows, units), (rows, units), (rows, 128)]
    args = [block, gain_half, w_gate, w_up]
    if before is None:
        return call(
            kernel,
            20,
            order,
            steps,
            in_specs,
            [whole(shape) for shape in sums],
            [jax.ShapeDtypeStruct(shape, F32) for shape in sums],
            [],
            *args,
        )
    return call(
        kernel,
        20,
        order,
        steps,
        in_specs + [whole(shape) for shape in sums],
        whole((rows, units)),
        jax.ShapeDtypeStruct((rows, units), BF16),
        [pltpu.VMEM(shape, F32) for shape in sums],
        *args,
        *before,
    )


def unpacker(slots, groups):
    row = jnp.arange(groups * slots, dtype=jnp.int32)
    low = row // slots * 2 * slots + row % slots
    place = jnp.concatenate([low, low + slots])
    return (place[:, None] == jnp.arange(groups * 2 * slots, dtype=jnp.int32)[None, :]).astype(BF16)


def packed_units(block, slots, groups, order, w_gate, w_up):
    packed, width = block.shape
    rows = packed // 2
    units = w_gate.shape[2]
    steps = width // STEP
    part = groups * slots
    pick = unpacker(slots, groups)
    per_slice = steps // 2

    def rows_of(k, order):
        step = k // 2
        return (0, order[k % 2 * 2 + step // per_slice] * per_slice + step % per_slice, 0)

    weights = pl.BlockSpec((1, STEP, units), rows_of)

    def kernel(order_ref, x_ref, pick_ref, wg_ref, wu_ref, act_ref, row_ref, gate_ref, up_ref):
        k = pl.program_id(0)

        @pl.when(k == 0)
        def _():
            gate_ref[...] = jnp.zeros_like(gate_ref)
            up_ref[...] = jnp.zeros_like(up_ref)

        @pl.when(k % 2 == 0)
        def _():
            for b in range(rows // part):
                both = dot(pick_ref[...], x_ref[2 * b * part : 2 * (b + 1) * part, :]).astype(BF16)
                row_ref[0, b * part : (b + 1) * part, :] = both[:part]
                row_ref[1, b * part : (b + 1) * part, :] = both[part:]

        x = row_ref[k % 2]
        gate_ref[...] += dot(x, wg_ref[0])
        up_ref[...] += dot(x, wu_ref[0])

        @pl.when(k == 2 * steps - 1)
        def _():
            act_ref[...] = gated(gate_ref[...], up_ref[...])

    return call(
        kernel,
        40,
        order,
        2 * steps,
        [
            pl.BlockSpec((packed, STEP), lambda k, order: (0, k // 2)),
            whole(pick.shape),
            weights,
            weights,
        ],
        whole((rows, units)),
        jax.ShapeDtypeStruct((rows, units), BF16),
        [pltpu.VMEM((2, rows, STEP), BF16)] + [pltpu.VMEM((rows, units), F32)] * 2,
        block,
        pick,
        w_gate,
        w_up,
    )


def packed_out(act, slots, groups, order, w_down, down_theirs):
    act_theirs = half_swap(act)
    rows, units = act.shape
    width = down_theirs[0].shape[1]
    per_slice = width // OUT_STEP
    part = groups * slots
    place = unpacker(slots, groups).T

    def kernel(order_ref, mine_ref, theirs_ref, place_ref, *refs):
        low_mine, high_mine, low_theirs, high_theirs, out_ref = refs
        low = dot(mine_ref[...], low_mine[0]) + dot(theirs_ref[...], low_theirs[...])
        high = dot(mine_ref[...], high_mine[0]) + dot(theirs_ref[...], high_theirs[...])
        low, high = low.astype(BF16), high.astype(BF16)
        for b in range(rows // part):
            here = slice(b * part, (b + 1) * part)
            both = dot(place_ref[...], jnp.concatenate([low[here], high[here]], axis=0))
            out_ref[2 * b * part : 2 * (b + 1) * part, :] = both.astype(BF16)

    def columns(number):
        return pl.BlockSpec((1, units, OUT_STEP), lambda k, order: (0, 0, order[number] * per_slice + k))

    return call(
        kernel,
        40,
        order,
        per_slice,
        [whole((rows, units)), whole((rows, units)), whole(place.shape), columns(0), columns(1)]
        + [pl.BlockSpec((units, OUT_STEP), lambda k, order: (0, k))] * 2,
        pl.BlockSpec((2 * rows, OUT_STEP), lambda k, order: (0, k)),
        jax.ShapeDtypeStruct((2 * rows, width), BF16),
        [],
        act,
        act_theirs,
        place,
        w_down,
        w_down,
        *down_theirs,
    )


def per_device(
    query_states,
    key_states,
    value_states,
    selected,
    residual,
    out_weight,
    norm_gain,
    w_gate,
    w_up,
    w_down,
    routes,
    route_weights,
):
    count = lax.axis_size("seq")
    exp = lax.axis_index("exp")
    rows, width = residual.shape
    heads = out_weight.shape[0]
    model_width = 4 * width
    group = exp // 2
    side = (exp >= 2).astype(jnp.int32)
    half = jnp.where(jnp.logical_or(exp == 0, exp == 3), 0, 1)
    other = 1 - half

    def ordered(mine, theirs):
        lower = side == 0
        return jnp.concatenate(
            [jnp.where(lower, mine, theirs), jnp.where(lower, theirs, mine)], axis=1
        )

    order = jnp.stack([half, 3 - half, other, 3 - other])
    theirs_order = jnp.stack([other, 3 - other, half, 3 - half])

    full_out = lax.all_gather(out_weight.reshape(-1, model_width), "seq", axis=0, tiled=True)
    gain = norm_gain[None, :]
    gain_mine = ordered(gain, group_swap(gain))
    gain_theirs = half_swap(gain_mine)
    residual_half = ordered(residual, group_swap(residual))

    down_given = [
        lax.dynamic_slice_in_dim(w_down[0], theirs_order[n] * width, width, 1) for n in range(2)
    ]
    down_given, gain_theirs = lax.optimization_barrier((down_given, gain_theirs))
    early = [half_swap(down_given[0]), half_swap(down_given[1][:EARLY])]

    experts = 2 * jnp.arange(count, dtype=jnp.int32) + group
    named = routes.T[:, None, :] == experts[None, :, None]
    hits = jnp.any(named, axis=0)
    token_weight = jnp.sum(jnp.where(named, route_weights.T[:, None, :].astype(F32), 0.0), axis=0)
    steps = jnp.arange(rows, dtype=jnp.int32)
    earlier = (steps[:, None] < steps[None, :]).astype(BF16)
    rank = jnp.where(hits, dot(hits.astype(BF16), earlier).astype(jnp.int32), -1)

    def slots(first, number):
        ids = first + jnp.arange(number, dtype=jnp.int32)
        return rank[:, None, :] == ids[None, :, None]

    def picker(mask):
        return mask.astype(BF16).reshape(-1, mask.shape[-1])

    def weigher(mask, high):
        empty = jnp.zeros_like(mask)
        mask = jnp.where(
            high,
            jnp.concatenate([empty, mask], axis=1),
            jnp.concatenate([mask, empty], axis=1),
        )
        return jnp.where(mask, token_weight[:, None, :], 0.0).astype(BF16).reshape(-1, rows)

    first = slots(0, SWAPPED)
    last = slots(SWAPPED, DIRECT)
    empty = jnp.zeros_like(last)
    pick_last = jnp.concatenate(
        [
            picker(jnp.concatenate([last, empty], axis=1)),
            picker(jnp.concatenate([empty, last], axis=1)),
        ],
        axis=1,
    )

    attended = attend(query_states, key_states, value_states, selected, heads)
    attended = regroup(attended, heads, count)
    late = [down_given[1][EARLY:MIDDLE], down_given[1][MIDDLE:]]
    attended, late, residual_half = lax.optimization_barrier((attended, late, residual_half))
    total, (late, early) = project_sum(
        attended, full_out, order, theirs_order, width, (late, early)
    )
    late = [half_swap(block) for block in late]
    hidden = (total + residual_half.astype(F32)).astype(BF16).astype(F32)
    gained = (hidden * gain_mine.astype(F32)).astype(BF16)
    gained, late[0] = lax.optimization_barrier((gained, late[0]))
    gained_other = half_swap(gained)

    received = spread(dot(picker(first), gained).astype(BF16))
    halves = [(gained, gain_mine), (gained_other, gain_theirs)]
    squares = sum(
        jnp.sum(jnp.square(block.astype(F32) / gain_half.astype(F32)), axis=1, keepdims=True)
        for block, gain_half in halves
    )
    scale = lax.rsqrt(squares / model_width + EPSILON)
    both = jnp.concatenate([(block.astype(F32) * scale).astype(BF16) for block, _ in halves], axis=0)
    rows_out = dot(pick_last, both).astype(BF16)
    rows_out, received, late[1] = lax.optimization_barrier((rows_out, received, late[1]))
    down_theirs = [early[0], jnp.concatenate([early[1], *late], axis=0)]
    received_last = spread(rows_out)

    before = half_units(received, gain_mine, order, w_gate, w_up)
    act = half_units(half_swap(received), gain_theirs, theirs_order, w_gate, w_up, before)
    first_out = packed_out(act, SWAPPED, 128 // SWAPPED, order, w_down, down_theirs)
    first_out, received_last = lax.optimization_barrier((first_out, received_last))
    first_out = spread(first_out)
    act = packed_units(received_last, DIRECT, 96 // DIRECT, order, w_gate, w_up)
    last_out = packed_out(act, DIRECT, 96 // DIRECT, order, w_down, down_theirs)
    last_out, first_out = lax.optimization_barrier((last_out, first_out))
    last_out = spread(last_out)

    high = side == 0
    give = dot_rows(weigher(first, high), first_out)
    keep = dot_rows(weigher(first, ~high), first_out)
    keep = keep + jnp.where(high, hidden[:, :width], hidden[:, width:])
    give_last, keep_last = weigher(last, high), weigher(last, ~high)
    last_out, give, keep, give_last, keep_last = lax.optimization_barrier(
        (last_out, give, keep, give_last, keep_last)
    )
    give = group_swap((give + dot_rows(give_last, last_out)).astype(BF16))
    keep = keep + dot_rows(keep_last, last_out)
    return (keep + give.astype(F32)).astype(BF16)


def solution(mesh):
    return jax.shard_map(
        per_device,
        mesh=mesh,
        in_specs=(
            P("seq", "exp"),
            P("seq", "exp"),
            P("seq", "exp"),
            P(),
            P("seq", "exp"),
            P("exp", "seq", None),
            P("exp"),
            P(("seq", "exp"), None, None),
            P(("seq", "exp"), None, None),
            P(("seq", "exp"), None, None),
            P("seq", None),
            P("seq", None),
        ),
        out_specs=P("seq", "exp"),
        check_vma=False,
    )
```

```python
import math

import jax
import jax.numpy as jnp
from jax import lax
from jax.experimental import pallas as pl
from jax.experimental.pallas import tpu as pltpu
from jax.sharding import PartitionSpec as P

EPSILON = 1e-06
NEGATIVE = -1e30
CAP = 20
DIRECT = 12
SWAPPED = CAP - DIRECT
EARLY = 208
MIDDLE = 320
STEP = 1792
OUT_STEP = 896
MIB = 2**20
BF16 = jnp.bfloat16
F32 = jnp.float32


def dot(a, b):
    return jnp.dot(a, b, preferred_element_type=F32)


def dot_rows(a, b):
    return lax.dot_general(a, b, (((0,), (0,)), ((), ())), preferred_element_type=F32)


def half_swap(block):
    return lax.ppermute(block, "exp", [(i, i ^ 1) for i in range(4)])


def group_swap(block):
    return lax.ppermute(block, "exp", [(i, 3 - i) for i in range(4)])


def spread(block):
    return lax.all_to_all(block, "seq", split_axis=0, concat_axis=0, tiled=True)


def fetch_blocks(key_states, value_states, selected):
    count = lax.axis_size("seq")
    rows, width = key_states.shape
    piece = 2 * rows // count
    stacked = jnp.concatenate([key_states, value_states], axis=0)
    pieces = spread(stacked).reshape(count, piece, width)
    previous = lax.ppermute(stacked, "seq", [(i, i + 1) for i in range(count - 1)])
    before = jnp.arange(count, dtype=jnp.int32)[:, None] - 1
    place = jnp.argmax(selected == before, axis=1)
    first = jnp.where(place == 0, selected[:, 1], selected[:, 0])
    second = jnp.where(place == 2, selected[:, 1], selected[:, 2])
    others = jnp.stack([first, second], axis=1)
    wanted = jnp.take(pieces, others.reshape(-1), axis=0).reshape(-1, width)
    fetched = spread(wanted)
    return fetched, previous, others


def attend(query_states, key_states, value_states, selected, heads):
    position = lax.axis_index("seq")
    rows, width = query_states.shape
    head_dim = width // heads
    fetched, previous, others = fetch_blocks(key_states, value_states, selected)
    keys = jnp.concatenate([fetched[: 2 * rows], previous[:rows], key_states], axis=0)
    values = jnp.concatenate([fetched[2 * rows :], previous[rows:], value_states], axis=0)
    keys = keys.reshape(-1, heads, head_dim)
    values = values.reshape(-1, heads, head_dim)
    queries = query_states.reshape(rows, heads, head_dim)
    scores = jnp.einsum("qhd,khd->hqk", queries, keys, preferred_element_type=F32) * (
        1.0 / math.sqrt(head_dim)
    )
    mine = lax.dynamic_slice_in_dim(others, position, 1, 0)[0] < position
    turn = jnp.arange(2 * rows, dtype=jnp.int32) // (2 * rows // lax.axis_size("seq")) % 2
    far = jnp.where(turn == 0, mine[0], mine[1])
    far = jnp.concatenate([far, jnp.broadcast_to(position > 0, (rows,))])
    places = jnp.arange(rows, dtype=jnp.int32)
    causal = places[None, :] <= places[:, None]
    visible = jnp.concatenate(
        [jnp.broadcast_to(far[None, :], (rows, far.shape[0])), causal], axis=1
    )
    scores = jnp.where(visible[None], scores, NEGATIVE)
    peak = jnp.max(scores, axis=2, keepdims=True)
    weights = jnp.exp(scores - peak)
    total = jnp.sum(weights, axis=2, keepdims=True)
    soft_weights = (weights / total).astype(BF16)
    attended = jnp.einsum("hqk,khd->qhd", soft_weights, values, preferred_element_type=F32)
    return attended.astype(BF16).reshape(rows, width)


def regroup(attended, heads, pieces):
    width = attended.shape[1]
    head_dim = width // heads
    piece = head_dim // pieces
    old = jnp.arange(width, dtype=jnp.int32)
    new_of_old = (old % head_dim) // piece * (heads * piece) + old // head_dim * piece + old % piece
    move = (new_of_old[:, None] == jnp.arange(width, dtype=jnp.int32)[None, :]).astype(BF16)
    return dot(attended, move).astype(BF16)


def project_sum(attended, full_out, order, theirs_order, width, behind):
    def product(index):
        columns = lax.dynamic_slice_in_dim(full_out, index * width, width, 1)
        return dot(attended, columns).astype(BF16)

    given = [half_swap(product(theirs_order[n])) for n in range(2)]
    kept = [product(order[n]) for n in range(2)]
    for n in range(2):
        given[n], kept[n] = lax.optimization_barrier((given[n], kept[n]))
    given[0], behind = lax.optimization_barrier((given[0], behind))
    pairs = [(a.astype(F32) + b.astype(F32)).astype(BF16) for a, b in zip(kept, given)]
    total = [pair.astype(F32) + group_swap(pair).astype(F32) for pair in pairs]
    return jnp.concatenate(total, axis=1), behind


def lane_sums(block):
    total = block[:, :128]
    for low in range(128, block.shape[1], 128):
        total = total + block[:, low : low + 128]
    return total


def gated(gate, up):
    return (gate / (1.0 + jnp.exp(-gate)) * up).astype(BF16)


def call(kernel, vmem, order, steps, in_specs, out_specs, out_shape, scratch, *args):
    return pl.pallas_call(
        kernel,
        grid_spec=pltpu.PrefetchScalarGridSpec(
            num_scalar_prefetch=1,
            grid=(steps,),
            in_specs=in_specs,
            out_specs=out_specs,
            scratch_shapes=scratch,
        ),
        out_shape=out_shape,
        compiler_params=pltpu.CompilerParams(
            dimension_semantics=("arbitrary",), vmem_limit_bytes=vmem * MIB
        ),
        cost_estimate=pl.CostEstimate(flops=1000, bytes_accessed=1000, transcendentals=0),
    )(order, *args)


def whole(shape):
    return pl.BlockSpec(shape, lambda k, order: (0,) * len(shape))


def weight_rows(per_slice, units):
    return pl.BlockSpec(
        (1, STEP, units), lambda k, order: (0, order[k // per_slice] * per_slice + k % per_slice, 0)
    )


def half_units(block, gain_half, order, w_gate, w_up, before=None):
    rows, width = block.shape
    units = w_gate.shape[2]
    steps = width // STEP

    def kernel(order_ref, x_ref, gain_ref, wg_ref, wu_ref, *refs):
        k = pl.program_id(0)
        if before is None:
            gate_ref, up_ref, square_ref = refs
        else:
            gate_in, up_in, square_in, act_ref, gate_ref, up_ref, square_ref = refs

        @pl.when(k == 0)
        def _():
            for ref, start in zip(
                (gate_ref, up_ref, square_ref), (None,) * 3 if before is None else refs[:3]
            ):
                ref[...] = jnp.zeros_like(ref) if start is None else start[...]

        x = x_ref[...]
        gate_ref[...] += dot(x, wg_ref[0])
        up_ref[...] += dot(x, wu_ref[0])
        plain = x.astype(F32) * (1.0 / gain_ref[...].astype(F32))
        square_ref[...] += lane_sums(plain * plain)
        if before is not None:

            @pl.when(k == steps - 1)
            def _():
                total = jnp.sum(square_ref[...], axis=1, keepdims=True)
                scale = lax.rsqrt(total / (2 * width) + EPSILON)
                act_ref[...] = gated(gate_ref[...] * scale, up_ref[...] * scale)

    per_slice = steps // 2
    in_specs = [
        pl.BlockSpec((rows, STEP), lambda k, order: (0, k)),
        pl.BlockSpec((1, STEP), lambda k, order: (0, k)),
        weight_rows(per_slice, units),
        weight_rows(per_slice, units),
    ]
    sums = [(rows, units), (rows, units), (rows, 128)]
    args = [block, gain_half, w_gate, w_up]
    if before is None:
        return call(
            kernel,
            20,
            order,
            steps,
            in_specs,
            [whole(shape) for shape in sums],
            [jax.ShapeDtypeStruct(shape, F32) for shape in sums],
            [],
            *args,
        )
    return call(
        kernel,
        20,
        order,
        steps,
        in_specs + [whole(shape) for shape in sums],
        whole((rows, units)),
        jax.ShapeDtypeStruct((rows, units), BF16),
        [pltpu.VMEM(shape, F32) for shape in sums],
        *args,
        *before,
    )


def unpacker(slots, groups):
    row = jnp.arange(groups * slots, dtype=jnp.int32)
    low = row // slots * 2 * slots + row % slots
    place = jnp.concatenate([low, low + slots])
    return (place[:, None] == jnp.arange(groups * 2 * slots, dtype=jnp.int32)[None, :]).astype(BF16)


def packed_units(block, slots, groups, order, w_gate, w_up):
    packed, width = block.shape
    rows = packed // 2
    units = w_gate.shape[2]
    steps = width // STEP
    part = groups * slots
    pick = unpacker(slots, groups)
    per_slice = steps // 2

    def rows_of(k, order):
        step = k // 2
        return (0, order[k % 2 * 2 + step // per_slice] * per_slice + step % per_slice, 0)

    weights = pl.BlockSpec((1, STEP, units), rows_of)

    def kernel(order_ref, x_ref, pick_ref, wg_ref, wu_ref, act_ref, row_ref, gate_ref, up_ref):
        k = pl.program_id(0)

        @pl.when(k == 0)
        def _():
            gate_ref[...] = jnp.zeros_like(gate_ref)
            up_ref[...] = jnp.zeros_like(up_ref)

        @pl.when(k % 2 == 0)
        def _():
            for b in range(rows // part):
                both = dot(pick_ref[...], x_ref[2 * b * part : 2 * (b + 1) * part, :]).astype(BF16)
                row_ref[0, b * part : (b + 1) * part, :] = both[:part]
                row_ref[1, b * part : (b + 1) * part, :] = both[part:]

        x = row_ref[k % 2]
        gate_ref[...] += dot(x, wg_ref[0])
        up_ref[...] += dot(x, wu_ref[0])

        @pl.when(k == 2 * steps - 1)
        def _():
            act_ref[...] = gated(gate_ref[...], up_ref[...])

    return call(
        kernel,
        58,
        order,
        2 * steps,
        [
            pl.BlockSpec((packed, STEP), lambda k, order: (0, k // 2)),
            whole(pick.shape),
            weights,
            weights,
        ],
        whole((rows, units)),
        jax.ShapeDtypeStruct((rows, units), BF16),
        [pltpu.VMEM((2, rows, STEP), BF16)] + [pltpu.VMEM((rows, units), F32)] * 2,
        block,
        pick,
        w_gate,
        w_up,
    )


def packed_out(act, slots, groups, order, w_down, down_theirs):
    act_theirs = half_swap(act)
    rows, units = act.shape
    width = down_theirs[0].shape[1]
    per_slice = width // OUT_STEP
    part = groups * slots
    place = unpacker(slots, groups).T

    def kernel(order_ref, mine_ref, theirs_ref, place_ref, *refs):
        low_mine, high_mine, low_theirs, high_theirs, out_ref = refs
        low = dot(mine_ref[...], low_mine[0]) + dot(theirs_ref[...], low_theirs[...])
        high = dot(mine_ref[...], high_mine[0]) + dot(theirs_ref[...], high_theirs[...])
        low, high = low.astype(BF16), high.astype(BF16)
        for b in range(rows // part):
            here = slice(b * part, (b + 1) * part)
            both = dot(place_ref[...], jnp.concatenate([low[here], high[here]], axis=0))
            out_ref[2 * b * part : 2 * (b + 1) * part, :] = both.astype(BF16)

    def columns(number):
        return pl.BlockSpec((1, units, OUT_STEP), lambda k, order: (0, 0, order[number] * per_slice + k))

    return call(
        kernel,
        40,
        order,
        per_slice,
        [whole((rows, units)), whole((rows, units)), whole(place.shape), columns(0), columns(1)]
        + [pl.BlockSpec((units, OUT_STEP), lambda k, order: (0, k))] * 2,
        pl.BlockSpec((2 * rows, OUT_STEP), lambda k, order: (0, k)),
        jax.ShapeDtypeStruct((2 * rows, width), BF16),
        [],
        act,
        act_theirs,
        place,
        w_down,
        w_down,
        *down_theirs,
    )


def per_device(
    query_states,
    key_states,
    value_states,
    selected,
    residual,
    out_weight,
    norm_gain,
    w_gate,
    w_up,
    w_down,
    routes,
    route_weights,
):
    count = lax.axis_size("seq")
    exp = lax.axis_index("exp")
    rows, width = residual.shape
    heads = out_weight.shape[0]
    model_width = 4 * width
    group = exp // 2
    side = (exp >= 2).astype(jnp.int32)
    half = jnp.where(jnp.logical_or(exp == 0, exp == 3), 0, 1)
    other = 1 - half

    def ordered(mine, theirs):
        lower = side == 0
        return jnp.concatenate(
            [jnp.where(lower, mine, theirs), jnp.where(lower, theirs, mine)], axis=1
        )

    order = jnp.stack([half, 3 - half, other, 3 - other])
    theirs_order = jnp.stack([other, 3 - other, half, 3 - half])

    full_out = lax.all_gather(out_weight.reshape(-1, model_width), "seq", axis=0, tiled=True)
    gain = norm_gain[None, :]
    gain_mine = ordered(gain, group_swap(gain))
    gain_theirs = half_swap(gain_mine)
    residual_half = ordered(residual, group_swap(residual))

    down_given = [
        lax.dynamic_slice_in_dim(w_down[0], theirs_order[n] * width, width, 1) for n in range(2)
    ]
    down_given, gain_theirs = lax.optimization_barrier((down_given, gain_theirs))
    early = [half_swap(down_given[0]), half_swap(down_given[1][:EARLY])]

    experts = 2 * jnp.arange(count, dtype=jnp.int32) + group
    named = routes.T[:, None, :] == experts[None, :, None]
    hits = jnp.any(named, axis=0)
    token_weight = jnp.sum(jnp.where(named, route_weights.T[:, None, :].astype(F32), 0.0), axis=0)
    steps = jnp.arange(rows, dtype=jnp.int32)
    earlier = (steps[:, None] < steps[None, :]).astype(BF16)
    rank = jnp.where(hits, dot(hits.astype(BF16), earlier).astype(jnp.int32), -1)

    def slots(first, number):
        ids = first + jnp.arange(number, dtype=jnp.int32)
        return rank[:, None, :] == ids[None, :, None]

    def picker(mask):
        return mask.astype(BF16).reshape(-1, mask.shape[-1])

    def weigher(mask, high):
        empty = jnp.zeros_like(mask)
        mask = jnp.where(
            high,
            jnp.concatenate([empty, mask], axis=1),
            jnp.concatenate([mask, empty], axis=1),
        )
        return jnp.where(mask, token_weight[:, None, :], 0.0).astype(BF16).reshape(-1, rows)

    first = slots(0, SWAPPED)
    last = slots(SWAPPED, DIRECT)
    empty = jnp.zeros_like(last)
    pick_last = jnp.concatenate(
        [
            picker(jnp.concatenate([last, empty], axis=1)),
            picker(jnp.concatenate([empty, last], axis=1)),
        ],
        axis=1,
    )

    attended = attend(query_states, key_states, value_states, selected, heads)
    attended = regroup(attended, heads, count)
    late = [down_given[1][EARLY:MIDDLE], down_given[1][MIDDLE:]]
    attended, late, residual_half = lax.optimization_barrier((attended, late, residual_half))
    total, (late, early) = project_sum(
        attended, full_out, order, theirs_order, width, (late, early)
    )
    late = [half_swap(block) for block in late]
    hidden = (total + residual_half.astype(F32)).astype(BF16).astype(F32)
    gained = (hidden * gain_mine.astype(F32)).astype(BF16)
    gained, late[0] = lax.optimization_barrier((gained, late[0]))
    gained_other = half_swap(gained)

    received = spread(dot(picker(first), gained).astype(BF16))
    halves = [(gained, gain_mine), (gained_other, gain_theirs)]
    squares = sum(
        jnp.sum(jnp.square(block.astype(F32) / gain_half.astype(F32)), axis=1, keepdims=True)
        for block, gain_half in halves
    )
    scale = lax.rsqrt(squares / model_width + EPSILON)
    both = jnp.concatenate([(block.astype(F32) * scale).astype(BF16) for block, _ in halves], axis=0)
    rows_out = dot(pick_last, both).astype(BF16)
    rows_out, received, late[1] = lax.optimization_barrier((rows_out, received, late[1]))
    down_theirs = [early[0], jnp.concatenate([early[1], *late], axis=0)]
    received_last = spread(rows_out)

    before = half_units(received, gain_mine, order, w_gate, w_up)
    act = half_units(half_swap(received), gain_theirs, theirs_order, w_gate, w_up, before)
    first_out = packed_out(act, SWAPPED, 128 // SWAPPED, order, w_down, down_theirs)
    first_out, received_last = lax.optimization_barrier((first_out, received_last))
    first_out = spread(first_out)
    act = packed_units(received_last, DIRECT, 96 // DIRECT, order, w_gate, w_up)
    last_out = packed_out(act, DIRECT, 96 // DIRECT, order, w_down, down_theirs)
    last_out, first_out = lax.optimization_barrier((last_out, first_out))
    last_out = spread(last_out)

    high = side == 0
    give = dot_rows(weigher(first, high), first_out)
    keep = dot_rows(weigher(first, ~high), first_out)
    keep = keep + jnp.where(high, hidden[:, :width], hidden[:, width:])
    give_last, keep_last = weigher(last, high), weigher(last, ~high)
    last_out, give, keep, give_last, keep_last = lax.optimization_barrier(
        (last_out, give, keep, give_last, keep_last)
    )
    give = group_swap((give + dot_rows(give_last, last_out)).astype(BF16))
    keep = keep + dot_rows(keep_last, last_out)
    return (keep + give.astype(F32)).astype(BF16)


def solution(mesh):
    return jax.shard_map(
        per_device,
        mesh=mesh,
        in_specs=(
            P("seq", "exp"),
            P("seq", "exp"),
            P("seq", "exp"),
            P(),
            P("seq", "exp"),
            P("exp", "seq", None),
            P("exp"),
            P(("seq", "exp"), None, None),
            P(("seq", "exp"), None, None),
            P(("seq", "exp"), None, None),
            P("seq", None),
            P("seq", None),
        ),
        out_specs=P("seq", "exp"),
        check_vma=False,
    )
```
